256 devices in a mesh: seq: 32 (over z, x), doc: 8 (over y, core).
Axes of the slice: x: 4, y: 4, z: 8, core: 2. Of those that a mesh axis runs over, the one named last changes fastest.
Arguments:
- queries: bfloat16 [24576, 4096], P(('doc', 'seq')), parts along dimension 0, may hold values from -250 to 250
- keys: bfloat16 [24576, 4096], P(('doc', 'seq')), parts along dimension 0, may hold values from -13 to 13
- values: bfloat16 [24576, 4096], P(('doc', 'seq')), parts along dimension 0, may hold values from -6 to 6
- fresh_queries: bfloat16 [24576, 4096], P(('doc', 'seq')), parts along dimension 0, may hold values from -250 to 250
- fresh_keys: bfloat16 [24576, 4096], P(('doc', 'seq')), parts along dimension 0, may hold values from -6 to 6
- fresh_values: bfloat16 [24576, 4096], P(('doc', 'seq')), parts along dimension 0, may hold values from -6 to 6
- masked_rows: int32 [256, 48], P(('doc', 'seq')), parts along dimension 0, may hold values from 0 to 95, as said below
- masked_counts: int32 [256], P(('doc', 'seq')), parts along dimension 0, may hold values from 1 to 48, as said below
Outputs:
- refresh_out: bfloat16 [24576, 4096], P(('doc', 'seq')), parts along dimension 0
- cached_out: bfloat16 [12288, 4096], P(('doc', 'seq')), parts along dimension 0
The draws below stay inside these ranges and needn't reach their ends.
There are 8 independent parts, one for each index of `doc`. The reference program is written for one: setup_inputs(seed, part) draws one part's arguments, and reference() takes and returns one part's arrays. A program takes and returns all parts, laid end to end along the dimension named above; each array names one. Nothing has to cross between parts.
Inputs may be any that keep to these rules, and one draw needn't show every extreme that they name: `masked_rows`: each shard's 48 entries are different positions of that shard; only the first masked_counts of them are still masked, the rest are ignored. `masked_counts`: some shard has all 48 slots live in every draw.
All inputs are finite; a program needn't handle non-finite values.
Results may differ from the reference program's by a relative error of at most 0.005.
Values may be sent and summed in bfloat16 or wider, within the bound.
A program may use at most 64 MiB of HBM per device.

```python
import math
import jax
import jax.numpy as jnp
from jax import lax

HEAD_DIM = 128
ROWS = 96
SLOTS = 48
HD = 4096
TOKENS = 3072


def scaled_keys(seed_key):
    base = jnp.clip(jax.random.normal(jax.random.fold_in(seed_key, 101), (TOKENS, HD), jnp.float32), -6.0, 6.0)
    return base


def draw_keys(key, part):
    drawn = scaled_keys(key)
    return drawn.astype(jnp.bfloat16)


def draw_queries(key, part):
    key = jax.random.fold_in(key, 2)
    entries = jnp.clip(jax.random.normal(key, (TOKENS, HD), jnp.float32), -6.0, 6.0)
    return entries.astype(jnp.bfloat16)


def draw_fresh_queries(key, part):
    key = jax.random.fold_in(key, 3)
    entries = jnp.clip(jax.random.normal(key, (TOKENS, HD), jnp.float32), -6.0, 6.0)
    return entries.astype(jnp.bfloat16)


def draw_masked_rows(key, part):
    key = jax.random.fold_in(key, 4)
    shards = TOKENS // ROWS
    shard_keys = jax.random.split(key, shards)
    orders = jax.vmap(lambda single: jax.random.permutation(single, ROWS))(shard_keys)
    return orders[:, :SLOTS].astype(jnp.int32)


def draw_masked_counts(key, part):
    key = jax.random.fold_in(key, 5)
    shards = TOKENS // ROWS
    counts = jax.random.randint(key, (shards,), 1, SLOTS + 1)
    busiest = jax.random.randint(jax.random.fold_in(key, 6), (), 0, shards)
    offset = jax.random.randint(jax.random.fold_in(key, 7), (), 1, shards)
    lighter = (busiest + offset) % shards
    light_count = jax.random.randint(jax.random.fold_in(key, 8), (), 1, SLOTS)
    counts = counts.at[lighter].set(light_count)
    return counts.at[busiest].set(SLOTS).astype(jnp.int32)


def level_of(stream_key, extent, cuts, least, largest):
    loudness = 1.0
    for dim, parts in cuts:
        steps = jax.random.uniform(jax.random.fold_in(jax.random.fold_in(stream_key, 6), dim), (parts,), jnp.float32, least / len(cuts), largest / len(cuts))
        loudness = loudness * jnp.repeat(jnp.exp(steps), extent[dim] // parts).reshape((-1,) + (1,) * (len(extent) - 1 - dim))
    return loudness


def noise(own_key, shape, scale, reach, pieces=(), kind=jnp.bfloat16):
    loudness = level_of(own_key, shape, pieces, -0.22, 0.18) if pieces else 1.0
    entries = jax.random.normal(own_key, shape, jnp.float32) * scale * loudness
    return jnp.minimum(jnp.maximum(entries, -reach), reach).astype(kind)


def setup_inputs(seed: int = 0, part: int = 0) -> dict:
    arg_keys = jax.random.split(jax.random.key(seed), 9)
    own_keys = jax.random.split(jax.random.fold_in(arg_keys[8], part), 9)
    return {
        "queries": draw_queries(jax.random.fold_in(jax.random.fold_in(arg_keys[8], part), 71), part),
        "keys": draw_keys(jax.random.fold_in(jax.random.fold_in(arg_keys[8], part), 71), part),
        "values": noise(own_keys[2], (TOKENS, HD), 1.0, 6.0, ((0, 32),)),
        "fresh_queries": draw_fresh_queries(jax.random.fold_in(jax.random.fold_in(arg_keys[8], part), 71), part),
        "fresh_keys": noise(own_keys[4], (TOKENS, HD), 1.0, 6.0, ((0, 32),)),
        "fresh_values": noise(own_keys[5], (TOKENS, HD), 1.0, 6.0, ((0, 32),)),
        "masked_rows": draw_masked_rows(jax.random.fold_in(jax.random.fold_in(arg_keys[8], part), 71), part),
        "masked_counts": draw_masked_counts(jax.random.fold_in(jax.random.fold_in(arg_keys[8], part), 71), part),
    }


def attend(query_rows, key_rows, value_rows):
    row_total, width_cols = query_rows.shape
    head_count = width_cols // HEAD_DIM
    block_rows = min(512, row_total)
    score_scale = 1.0 / math.sqrt(HEAD_DIM)
    key_heads = key_rows.astype(jnp.float32).reshape(-1, head_count, HEAD_DIM)
    value_heads = value_rows.astype(jnp.float32).reshape(-1, head_count, HEAD_DIM)
    blocks_in = query_rows.reshape(row_total // block_rows, block_rows, head_count, HEAD_DIM)

    def one_block(query_block):
        scores = jnp.einsum('qhd,khd->hqk', query_block.astype(jnp.float32), key_heads) * score_scale
        row_top = lax.optimization_barrier(jnp.max(scores, axis=-1, keepdims=True))
        powers = jnp.exp(scores - row_top)
        weights = (powers / lax.optimization_barrier(jnp.sum(powers, axis=-1, keepdims=True))).astype(jnp.bfloat16)
        mixed = jnp.einsum('hqk,khd->qhd', weights.astype(jnp.float32), value_heads)
        return mixed.astype(jnp.bfloat16).reshape(block_rows, width_cols)
    return lax.map(one_block, blocks_in).reshape(row_total, width_cols)

def reference(queries, keys, values, fresh_queries, fresh_keys, fresh_values, masked_rows, masked_counts):
    refresh_out = attend(queries, keys, values)
    shard_ids = jnp.arange(masked_rows.shape[0], dtype=jnp.int32)
    positions = (shard_ids[:, None] * ROWS + masked_rows).reshape(-1).astype(jnp.int32)
    live_slots = (jnp.arange(SLOTS, dtype=jnp.int32)[None, :] < masked_counts[:, None]).reshape(-1)
    target = jnp.where(live_slots, positions, TOKENS).astype(jnp.int32)
    cache_keys = keys.at[target].set(fresh_keys[positions], mode='drop')
    cache_values = values.at[target].set(fresh_values[positions], mode='drop')
    cached = attend(fresh_queries[positions], cache_keys, cache_values)
    cached_out = jnp.where(live_slots[:, None], cached, jnp.zeros((), jnp.bfloat16))
    return (refresh_out, cached_out)
```

```python
import functools
import math

import jax
import jax.numpy as jnp
from jax import lax
from jax.experimental import pallas as pl
from jax.experimental.pallas import tpu as pltpu
from jax.sharding import PartitionSpec as P

HEAD_DIM = 128
MESH = pl.DeviceIdType.MESH
KEY_CHUNK = 512
EXP2_SCALE = math.log2(math.e) / math.sqrt(HEAD_DIM)


def attend(query_block, key_ref, value_ref, score_ref):
    tokens = key_ref.shape[0]
    rows = query_block.shape[0]
    top = None
    for c in range(0, tokens, KEY_CHUNK):
        scores = lax.dot_general(
            query_block,
            key_ref[pl.ds(c, KEY_CHUNK), :],
            (((1,), (1,)), ((), ())),
            preferred_element_type=jnp.float32,
        )
        score_ref[:, pl.ds(c, KEY_CHUNK)] = scores
        for g in range(0, KEY_CHUNK, HEAD_DIM):
            part = scores[:, g : g + HEAD_DIM]
            top = part if top is None else jnp.maximum(top, part)
    top = jnp.max(top, axis=-1, keepdims=True)
    total = jnp.zeros((rows, 2 * HEAD_DIM), jnp.float32)
    for c in range(0, tokens, KEY_CHUNK):
        powers = jnp.exp2((score_ref[:, pl.ds(c, KEY_CHUNK)] - top) * EXP2_SCALE)
        total += jnp.dot(
            powers.astype(jnp.bfloat16),
            value_ref[pl.ds(c, KEY_CHUNK), :],
            preferred_element_type=jnp.float32,
        )
    return total[:, :HEAD_DIM] / total[:, HEAD_DIM:]


def kernel(
    shards,
    q_ref,
    k_ref,
    v_ref,
    fq_ref,
    fk_ref,
    fv_ref,
    rows_ref,
    count_ref,
    refresh_ref,
    cached_ref,
    q_buf,
    k_buf,
    v_buf,
    fresh_own,
    fresh_out,
    fresh_buf,
    list_out,
    list_buf,
    score_buf,
    refresh_buf,
    cached_buf,
    load_sem,
    send_sem,
    recv_sem,
):
    me = lax.axis_index("seq")
    own = q_ref.shape[0]
    slots = rows_ref.shape[1]

    def peer(i):
        return lax.rem(me + i, shards)

    def columns(head):
        return pl.ds(pl.multiple_of(head * HEAD_DIM, HEAD_DIM), HEAD_DIM)

    def rows_of(shard):
        return pl.ds(pl.multiple_of(shard * own, own), own)

    loads = [
        pltpu.make_async_copy(ref, fresh_own.at[i], load_sem.at[i])
        for i, ref in enumerate((fq_ref, fk_ref, fv_ref))
    ]
    for load in loads:
        load.start()

    barrier = pltpu.get_barrier_semaphore()

    def greet(i, carry):
        pl.semaphore_signal(barrier, inc=1, device_id={"seq": peer(i)}, device_id_type=MESH)
        return carry

    lax.fori_loop(1, shards, greet, 0)
    pl.semaphore_wait(barrier, shards - 1)

    stage_a = ((k_ref, k_buf, 0), (v_ref, v_buf, 1), (q_ref, q_buf, 2))

    def send_a(i, carry):
        to = peer(i)
        for ref, buf, n in stage_a:
            pltpu.make_async_remote_copy(
                src_ref=ref.at[:, columns(to)],
                dst_ref=buf.at[rows_of(me), pl.ds(0, HEAD_DIM)],
                send_sem=send_sem.at[n],
                recv_sem=recv_sem.at[n],
                device_id={"seq": to},
                device_id_type=MESH,
            ).start()
        return carry

    lax.fori_loop(1, shards, send_a, 0)
    for ref, buf, n in stage_a:
        pltpu.make_async_copy(
            ref.at[:, columns(me)], buf.at[rows_of(me), pl.ds(0, HEAD_DIM)], recv_sem.at[n]
        ).start()

    count = count_ref[0]
    listed = rows_ref[...]
    lane = lax.broadcasted_iota(jnp.int32, (1, slots), 1)
    list_out[...] = jnp.full(list_out.shape, count, jnp.int32)
    list_out[0:1, 0:slots] = jnp.where(lane < count, listed, -1)
    pick = (lax.broadcasted_iota(jnp.int32, (own, slots), 0) == listed).astype(jnp.float32)
    pick = jnp.transpose(pick).astype(jnp.bfloat16)
    for load in loads:
        load.wait()

    def gather(head, carry):
        for i in range(3):
            fresh_out[head, :, pl.ds(i * HEAD_DIM, HEAD_DIM)] = jnp.dot(
                pick, fresh_own[i, :, columns(head)], preferred_element_type=jnp.float32
            ).astype(jnp.bfloat16)
        return carry

    lax.fori_loop(0, shards, gather, 0)

    def send_b(i, carry):
        to = peer(i)
        for src, dst, n in (
            (fresh_out.at[to], fresh_buf.at[me], 3),
            (list_out, list_buf.at[me], 4),
        ):
            pltpu.make_async_remote_copy(
                src_ref=src,
                dst_ref=dst,
                send_sem=send_sem.at[n],
                recv_sem=recv_sem.at[n],
                device_id={"seq": to},
                device_id_type=MESH,
            ).start()
        return carry

    lax.fori_loop(1, shards, send_b, 0)
    pltpu.make_async_copy(fresh_out.at[me], fresh_buf.at[me], recv_sem.at[3]).start()
    pltpu.make_async_copy(list_out, list_buf.at[me], recv_sem.at[4]).start()

    v_buf[:, HEAD_DIM:] = jnp.ones((v_buf.shape[0], HEAD_DIM), jnp.bfloat16)

    def arrived(ref, n):
        pltpu.make_async_copy(ref, ref, recv_sem.at[n]).wait()

    arrived(k_buf, 0)
    arrived(v_buf.at[:, pl.ds(0, HEAD_DIM)], 1)
    arrived(q_buf, 2)

    def send_home(src, dst, to, n):
        @pl.when(to != me)
        def _():
            pltpu.make_async_remote_copy(
                src_ref=src,
                dst_ref=dst,
                send_sem=send_sem.at[n],
                recv_sem=recv_sem.at[n],
                device_id={"seq": to},
                device_id_type=MESH,
            ).start()

        @pl.when(to == me)
        def _():
            pltpu.make_async_copy(src, dst, recv_sem.at[n]).start()

    def refresh(i, carry):
        block = pl.ds(pl.multiple_of(i * 2 * own, 2 * own), 2 * own)
        out = attend(q_buf[block, :], k_buf, v_buf, score_buf)
        refresh_buf[block, :] = out.astype(jnp.bfloat16)
        for j in range(2):
            to = 2 * i + j
            send_home(refresh_buf.at[rows_of(to)], refresh_ref.at[:, columns(me)], to, 5)
        return carry

    lax.fori_loop(0, shards // 2, refresh, 0)

    arrived(fresh_buf, 3)
    arrived(list_buf, 4)

    def update(shard, carry):
        at = list_buf[shard, 0:1, 0:slots]
        put = lax.broadcasted_iota(jnp.int32, (own, slots), 0) == at
        put = put.astype(jnp.float32)
        changed = jnp.max(put, axis=-1, keepdims=True) > 0.0
        new = jnp.dot(
            put.astype(jnp.bfloat16),
            fresh_buf[shard, :, HEAD_DIM:],
            preferred_element_type=jnp.float32,
        ).astype(jnp.bfloat16)
        block = rows_of(shard)
        k_buf[block, :] = jnp.where(changed, new[:, :HEAD_DIM], k_buf[block, :])
        v_buf[block, :HEAD_DIM] = jnp.where(
            changed, new[:, HEAD_DIM:], v_buf[block, :HEAD_DIM]
        )
        return carry

    lax.fori_loop(0, shards, update, 0)

    def cached(i, carry):
        group = pl.ds(4 * i, 4)
        query_block = fresh_buf[group, :, 0:HEAD_DIM].reshape(4 * slots, HEAD_DIM)
        out = attend(query_block, k_buf, v_buf, score_buf)
        out = out.reshape(4, slots, HEAD_DIM)
        slot = lax.broadcasted_iota(jnp.int32, out.shape, 1)
        live = slot < list_buf[group, 1:2, :]
        cached_buf[group, :, :] = jnp.where(live, out, 0.0).astype(jnp.bfloat16)
        for j in range(4):
            to = 4 * i + j
            send_home(cached_buf.at[to], cached_ref.at[:, columns(me)], to, 6)
        return carry

    lax.fori_loop(0, shards // 4, cached, 0)

    arrived(refresh_ref, 5)
    arrived(cached_ref, 6)

    def sent(ref, n):
        pltpu.make_async_copy(ref, ref, send_sem.at[n]).wait()

    others = pl.ds(0, (shards - 1) * own)
    for n in (0, 1, 2, 5):
        sent(q_buf.at[others, :], n)
    sent(fresh_buf.at[pl.ds(0, shards - 1)], 3)
    sent(list_buf.at[pl.ds(0, shards - 1)], 4)
    sent(cached_buf.at[pl.ds(0, shards - 1)], 6)


def per_device(
    queries, keys, values, fresh_queries, fresh_keys, fresh_values, masked_rows, masked_counts
):
    own, width = queries.shape
    slots = masked_rows.shape[1]
    shards = lax.axis_size("seq")
    tokens = shards * own
    bf16 = jnp.bfloat16
    hbm = pl.BlockSpec(memory_space=pl.ANY)
    return pl.pallas_call(
        functools.partial(kernel, shards),
        name="attention",
        out_shape=(
            jax.ShapeDtypeStruct((own, width), bf16),
            jax.ShapeDtypeStruct((slots, width), bf16),
        ),
        in_specs=[hbm] * 6
        + [pl.BlockSpec(memory_space=pltpu.VMEM), pl.BlockSpec(memory_space=pltpu.SMEM)],
        out_specs=(hbm, hbm),
        scratch_shapes=[
            pltpu.VMEM((tokens, HEAD_DIM), bf16),
            pltpu.VMEM((tokens, HEAD_DIM), bf16),
            pltpu.VMEM((tokens, 2 * HEAD_DIM), bf16),
            pltpu.VMEM((3, own, width), bf16),
            pltpu.VMEM((shards, slots, 3 * HEAD_DIM), bf16),
            pltpu.VMEM((shards, slots, 3 * HEAD_DIM), bf16),
            pltpu.VMEM((2, HEAD_DIM), jnp.int32),
            pltpu.VMEM((shards, 2, HEAD_DIM), jnp.int32),
            pltpu.VMEM((2 * own, tokens), jnp.float32),
            pltpu.VMEM((tokens, HEAD_DIM), bf16),
            pltpu.VMEM((shards, slots, HEAD_DIM), bf16),
            pltpu.SemaphoreType.DMA((3,)),
            pltpu.SemaphoreType.DMA((7,)),
            pltpu.SemaphoreType.DMA((7,)),
        ],
        compiler_params=pltpu.CompilerParams(
            collective_id=0, has_side_effects=True, vmem_limit_bytes=40 * 2**20
        ),
        cost_estimate=pl.CostEstimate(
            flops=6 * tokens * tokens * HEAD_DIM,
            bytes_accessed=12 * own * width,
            transcendentals=tokens * tokens * 3 // 2,
        ),
    )(
        queries,
        keys,
        values,
        fresh_queries,
        fresh_keys,
        fresh_values,
        masked_rows,
        masked_counts,
    )


def solution(mesh):
    spread = P(("doc", "seq"), None)
    return jax.shard_map(
        per_device,
        mesh=mesh,
        in_specs=(spread,) * 7 + (P(("doc", "seq")),),
        out_specs=(spread, spread),
        check_vma=False,
    )
```

```python
import functools
import math

import jax
import jax.numpy as jnp
from jax import lax
from jax.experimental import pallas as pl
from jax.experimental.pallas import tpu as pltpu
from jax.sharding import PartitionSpec as P

HEAD_DIM = 128
PLANES = 8
VMEM_LIMIT = 105 * 2**19
MESH = pl.DeviceIdType.MESH
KEY_CHUNK = 256
EXP2_SCALE = math.log2(math.e) / math.sqrt(HEAD_DIM)


def attend(query_block, key_ref, value_ref):
    rows = query_block.shape[0]
    top = jnp.full((rows, 1), -jnp.inf, jnp.float32)
    total = jnp.zeros((rows, 2 * HEAD_DIM), jnp.float32)
    for c in range(0, key_ref.shape[0], KEY_CHUNK):
        scores = lax.dot_general(
            query_block,
            key_ref[pl.ds(c, KEY_CHUNK), :],
            (((1,), (1,)), ((), ())),
            preferred_element_type=jnp.float32,
        )
        new_top = jnp.maximum(top, jnp.max(scores, axis=-1, keepdims=True))
        powers = jnp.exp2((scores - new_top) * EXP2_SCALE).astype(jnp.bfloat16)
        total = total * jnp.exp2((top - new_top) * EXP2_SCALE) + jnp.dot(
            powers, value_ref[pl.ds(c, KEY_CHUNK), :], preferred_element_type=jnp.float32
        )
        top = new_top
    return total[:, :HEAD_DIM] / total[:, HEAD_DIM:]


def kernel(
    shards,
    q_ref,
    k_ref,
    v_ref,
    fq_ref,
    fk_ref,
    fv_ref,
    rows_ref,
    count_ref,
    refresh_ref,
    cached_ref,
    q_buf,
    k_buf,
    v_buf,
    fresh_own,
    fresh_out,
    fresh_buf,
    list_out,
    list_buf,
    refresh_buf,
    cached_buf,
    load_sem,
    send_sem,
    recv_sem,
):
    me = lax.axis_index("seq")
    width = shards // PLANES
    own = q_ref.shape[0]
    slots = rows_ref.shape[1]

    def plane(i):
        step = PLANES // 2 + lax.div(i + 1, 2) * (1 - 2 * lax.rem(i, 2))
        return lax.rem(lax.div(me, width) + step, PLANES)

    def peer(i):
        reach = PLANES - 1
        far = lax.div(i, reach) < width
        step = jnp.where(far, lax.div(i, reach) + 1, i - reach * width + 1)
        x = lax.rem(lax.rem(me, width) + step, width)
        return plane(jnp.where(far, lax.rem(i, reach), reach)) * width + x

    def columns(head):
        return pl.ds(pl.multiple_of(head * HEAD_DIM, HEAD_DIM), HEAD_DIM)

    def rows_of(shard):
        return pl.ds(pl.multiple_of(shard * own, own), own)

    loads = [
        pltpu.make_async_copy(ref, fresh_own.at[i], load_sem.at[i])
        for i, ref in enumerate((fq_ref, fk_ref, fv_ref))
    ]
    for load in loads:
        load.start()

    barrier = pltpu.get_barrier_semaphore()

    def greet(i, carry):
        pl.semaphore_signal(barrier, inc=1, device_id={"seq": peer(i)}, device_id_type=MESH)
        return carry

    lax.fori_loop(0, shards - 1, greet, 0)
    pl.semaphore_wait(barrier, shards - 1)

    stage_a = ((k_ref, k_buf, 0), (v_ref, v_buf, 1), (q_ref, q_buf, 2))

    for ref, buf, n in stage_a:

        def send_a(i, carry):
            to = peer(i)
            pltpu.make_async_remote_copy(
                src_ref=ref.at[:, columns(to)],
                dst_ref=buf.at[rows_of(me), pl.ds(0, HEAD_DIM)],
                send_sem=send_sem.at[n],
                recv_sem=recv_sem.at[n],
                device_id={"seq": to},
                device_id_type=MESH,
            ).start()
            return carry

        lax.fori_loop(0, shards - 1, send_a, 0)
    for ref, buf, n in stage_a:
        pltpu.make_async_copy(
            ref.at[:, columns(me)], buf.at[rows_of(me), pl.ds(0, HEAD_DIM)], recv_sem.at[n]
        ).start()

    count = count_ref[0]
    lane = lax.broadcasted_iota(jnp.int32, (1, slots), 1)
    listed = jnp.zeros((1, slots), jnp.int32)
    for j in range(slots):
        listed = jnp.where(lane == j, rows_ref[0, j], listed)
    list_out[...] = jnp.full(list_out.shape, count, jnp.int32)
    list_out[0:1, 0:slots] = jnp.where(lane < count, listed, -1)
    pick = (lax.broadcasted_iota(jnp.int32, (own, slots), 0) == listed).astype(jnp.float32)
    pick = jnp.transpose(pick).astype(jnp.bfloat16)
    for load in loads:
        load.wait()

    def gather(head, carry):
        for i in range(3):
            fresh_out[head, :, pl.ds(i * HEAD_DIM, HEAD_DIM)] = jnp.dot(
                pick, fresh_own[i, :, columns(head)], preferred_element_type=jnp.float32
            ).astype(jnp.bfloat16)
        return carry

    lax.fori_loop(0, shards, gather, 0)

    def send_b(i, carry):
        to = peer(i)
        for src, dst, n in (
            (fresh_out.at[to], fresh_buf.at[me], 3),
            (list_out, list_buf.at[me], 4),
        ):
            pltpu.make_async_remote_copy(
                src_ref=src,
                dst_ref=dst,
                send_sem=send_sem.at[n],
                recv_sem=recv_sem.at[n],
                device_id={"seq": to},
                device_id_type=MESH,
            ).start()
        return carry

    lax.fori_loop(0, shards - 1, send_b, 0)
    pltpu.make_async_copy(fresh_out.at[me], fresh_buf.at[me], recv_sem.at[3]).start()
    pltpu.make_async_copy(list_out, list_buf.at[me], recv_sem.at[4]).start()

    v_buf[:, HEAD_DIM:] = jnp.ones((v_buf.shape[0], HEAD_DIM), jnp.bfloat16)

    def arrived(ref, n):
        pltpu.make_async_copy(ref, ref, recv_sem.at[n]).wait()

    arrived(k_buf, 0)
    arrived(v_buf.at[:, pl.ds(0, HEAD_DIM)], 1)
    arrived(q_buf, 2)

    def send_home(src, dst, to, n):
        @pl.when(to != me)
        def _():
            pltpu.make_async_remote_copy(
                src_ref=src,
                dst_ref=dst,
                send_sem=send_sem.at[n],
                recv_sem=recv_sem.at[n],
                device_id={"seq": to},
                device_id_type=MESH,
            ).start()

        @pl.when(to == me)
        def _():
            pltpu.make_async_copy(src, dst, recv_sem.at[n]).start()

    def refresh(i, carry):
        first = plane(i) * width
        block = pl.ds(pl.multiple_of(first * own, width * own), width * own)
        out = attend(q_buf[block, :], k_buf, v_buf)
        refresh_buf[block, :] = out.astype(jnp.bfloat16)
        for j in range(width):
            to = first + j
            send_home(refresh_buf.at[rows_of(to)], refresh_ref.at[:, columns(me)], to, 5)
        return carry

    lax.fori_loop(0, PLANES, refresh, 0)

    arrived(fresh_buf, 3)
    arrived(list_buf, 4)

    def update(i, carry):
        for j in range(width):
            shard = i * width + j
            at = list_buf[shard, 0:1, 0:slots]
            put = lax.broadcasted_iota(jnp.int32, (own, slots), 0) == at
            put = put.astype(jnp.float32)
            changed = jnp.max(put, axis=-1, keepdims=True) > 0.0
            new = jnp.dot(
                put.astype(jnp.bfloat16),
                fresh_buf[shard, :, HEAD_DIM:],
                preferred_element_type=jnp.float32,
            ).astype(jnp.bfloat16)
            block = rows_of(shard)
            k_buf[block, :] = jnp.where(changed, new[:, :HEAD_DIM], k_buf[block, :])
            v_buf[block, :HEAD_DIM] = jnp.where(
                changed, new[:, HEAD_DIM:], v_buf[block, :HEAD_DIM]
            )
        return carry

    lax.fori_loop(0, PLANES, update, 0)

    def cached(i, carry):
        firsts = [plane(2 * i + j) * width for j in range(2)]
        groups = [pl.ds(first, width) for first in firsts]
        query_block = jnp.concatenate([fresh_buf[g, :, 0:HEAD_DIM] for g in groups])
        out = attend(query_block.reshape(-1, HEAD_DIM), k_buf, v_buf)
        out = out.reshape(2, width, slots, HEAD_DIM)
        slot = lax.broadcasted_iota(jnp.int32, out.shape[1:], 1)
        for j, group in enumerate(groups):
            live = slot < list_buf[group, 1:2, :]
            cached_buf[group, :, :] = jnp.where(live, out[j], 0.0).astype(jnp.bfloat16)
        for first in firsts:
            for j in range(width):
                to = first + j
                send_home(cached_buf.at[to], cached_ref.at[:, columns(me)], to, 6)
        return carry

    lax.fori_loop(0, PLANES // 2, cached, 0)

    arrived(refresh_ref, 5)
    arrived(cached_ref, 6)

    def sent(ref, n):
        pltpu.make_async_copy(ref, ref, send_sem.at[n]).wait()

    others = pl.ds(0, (shards - 1) * own)
    for n in (0, 1, 2, 5):
        sent(q_buf.at[others, :], n)
    sent(fresh_buf.at[pl.ds(0, shards - 1)], 3)
    sent(list_buf.at[pl.ds(0, shards - 1)], 4)
    sent(cached_buf.at[pl.ds(0, shards - 1)], 6)


def per_device(
    queries, keys, values, fresh_queries, fresh_keys, fresh_values, masked_rows, masked_counts
):
    own, width = queries.shape
    slots = masked_rows.shape[1]
    shards = lax.axis_size("seq")
    tokens = shards * own
    bf16 = jnp.bfloat16
    hbm = pl.BlockSpec(memory_space=pltpu.HBM)
    anywhere = pl.BlockSpec(memory_space=pl.ANY)
    return pl.pallas_call(
        functools.partial(kernel, shards),
        name="attention",
        out_shape=(
            jax.ShapeDtypeStruct((own, width), bf16),
            jax.ShapeDtypeStruct((slots, width), bf16),
        ),
        in_specs=[hbm] * 6 + [pl.BlockSpec(memory_space=pltpu.SMEM)] * 2,
        out_specs=(anywhere, anywhere),
        scratch_shapes=[
            pltpu.VMEM((tokens, HEAD_DIM), bf16),
            pltpu.VMEM((tokens, HEAD_DIM), bf16),
            pltpu.VMEM((tokens, 2 * HEAD_DIM), bf16),
            pltpu.VMEM((3, own, width), bf16),
            pltpu.VMEM((shards, slots, 3 * HEAD_DIM), bf16),
            pltpu.VMEM((shards, slots, 3 * HEAD_DIM), bf16),
            pltpu.VMEM((2, HEAD_DIM), jnp.int32),
            pltpu.VMEM((shards, 2, HEAD_DIM), jnp.int32),
            pltpu.VMEM((tokens, HEAD_DIM), bf16),
            pltpu.VMEM((shards, slots, HEAD_DIM), bf16),
            pltpu.SemaphoreType.DMA((3,)),
            pltpu.SemaphoreType.DMA((7,)),
            pltpu.SemaphoreType.DMA((7,)),
        ],
        compiler_params=pltpu.CompilerParams(
            collective_id=0, has_side_effects=True, vmem_limit_bytes=VMEM_LIMIT
        ),
        cost_estimate=pl.CostEstimate(
            flops=6 * tokens * tokens * HEAD_DIM,
            bytes_accessed=12 * own * width,
            transcendentals=tokens * tokens * 3 // 2,
        ),
    )(
        queries,
        keys,
        values,
        fresh_queries,
        fresh_keys,
        fresh_values,
        masked_rows,
        masked_counts,
    )


def solution(mesh):
    spread = P(("doc", "seq"), None)
    return jax.shard_map(
        per_device,
        mesh=mesh,
        in_specs=(spread,) * 7 + (P(("doc", "seq")),),
        out_specs=(spread, spread),
        check_vma=False,
    )
```

```python
import functools
import math

import jax
import jax.numpy as jnp
from jax import lax
from jax.experimental import pallas as pl
from jax.experimental.pallas import tpu as pltpu
from jax.sharding import PartitionSpec as P

HEAD_DIM = 128
PLANES = 8
VMEM_LIMIT = 105 * 2**19
MESH = pl.DeviceIdType.MESH
KEY_CHUNK = 256
EXP2_SCALE = math.log2(math.e) / math.sqrt(HEAD_DIM)


def attend(query_block, key_ref, value_ref):
    rows = query_block.shape[0]
    top = jnp.full((rows, 1), -jnp.inf, jnp.float32)
    total = jnp.zeros((rows, 2 * HEAD_DIM), jnp.float32)
    for c in range(0, key_ref.shape[0], KEY_CHUNK):
        scores = lax.dot_general(
            query_block,
            key_ref[pl.ds(c, KEY_CHUNK), :],
            (((1,), (1,)), ((), ())),
            preferred_element_type=jnp.float32,
        )
        new_top = jnp.maximum(top, jnp.max(scores, axis=-1, keepdims=True))
        powers = jnp.exp2((scores - new_top) * EXP2_SCALE).astype(jnp.bfloat16)
        total = total * jnp.exp2((top - new_top) * EXP2_SCALE) + jnp.dot(
            powers, value_ref[pl.ds(c, KEY_CHUNK), :], preferred_element_type=jnp.float32
        )
        top = new_top
    return total[:, :HEAD_DIM] / total[:, HEAD_DIM:]


def kernel(
    shards,
    q_ref,
    k_ref,
    v_ref,
    fq_ref,
    fk_ref,
    fv_ref,
    rows_ref,
    count_ref,
    refresh_ref,
    cached_ref,
    q_buf,
    k_buf,
    v_buf,
    fresh_own,
    fresh_out,
    fresh_buf,
    list_out,
    list_buf,
    refresh_buf,
    cached_buf,
    load_sem,
    send_sem,
    recv_sem,
):
    me = lax.axis_index("seq")
    width = shards // PLANES
    own = q_ref.shape[0]
    slots = rows_ref.shape[1]

    def plane(i):
        step = PLANES // 2 + lax.div(i + 1, 2) * (1 - 2 * lax.rem(i, 2))
        return lax.rem(lax.div(me, width) + step, PLANES)

    def peer(i):
        reach = PLANES - 1
        far = lax.div(i, reach) < width
        step = jnp.where(far, lax.div(i, reach) + 1, i - reach * width + 1)
        x = lax.rem(lax.rem(me, width) + step, width)
        return plane(jnp.where(far, lax.rem(i, reach), reach)) * width + x

    def early_plane(i):
        half = PLANES // 2
        turn = lax.rem(i, half)
        step = half // 2 + lax.div(turn + 1, 2) * (1 - 2 * lax.rem(turn, 2))
        return lax.div(i, half) * half + lax.rem(lax.rem(lax.div(me, width), half) + step, half)

    def columns(head):
        return pl.ds(pl.multiple_of(head * HEAD_DIM, HEAD_DIM), HEAD_DIM)

    def rows_of(shard):
        return pl.ds(pl.multiple_of(shard * own, own), own)

    barrier = pltpu.get_barrier_semaphore()

    def greet(i, carry):
        pl.semaphore_signal(barrier, inc=1, device_id={"seq": peer(i)}, device_id_type=MESH)
        return carry

    lax.fori_loop(0, shards - 1, greet, 0)
    loads = [
        pltpu.make_async_copy(ref, fresh_own.at[i], load_sem.at[i])
        for i, ref in enumerate((fq_ref, fk_ref, fv_ref))
    ]
    for load in loads:
        load.start()

    pl.semaphore_wait(barrier, shards - 1)

    stage_a = ((k_ref, k_buf, 0), (v_ref, v_buf, 1), (q_ref, q_buf, 2))

    for ref, buf, n in stage_a:

        def send_a(i, carry):
            to = peer(i)
            pltpu.make_async_remote_copy(
                src_ref=ref.at[:, columns(to)],
                dst_ref=buf.at[rows_of(me), pl.ds(0, HEAD_DIM)],
                send_sem=send_sem.at[n],
                recv_sem=recv_sem.at[n],
                device_id={"seq": to},
                device_id_type=MESH,
            ).start()
            return carry

        lax.fori_loop(0, shards - 1, send_a, 0)
    for ref, buf, n in stage_a:
        pltpu.make_async_copy(
            ref.at[:, columns(me)], buf.at[rows_of(me), pl.ds(0, HEAD_DIM)], recv_sem.at[n]
        ).start()

    count = count_ref[0]
    lane = lax.broadcasted_iota(jnp.int32, (1, slots), 1)
    listed = jnp.zeros((1, slots), jnp.int32)
    for j in range(slots):
        listed = jnp.where(lane == j, rows_ref[0, j], listed)
    list_out[...] = jnp.full(list_out.shape, count, jnp.int32)
    list_out[0:1, 0:slots] = jnp.where(lane < count, listed, -1)
    pick = (lax.broadcasted_iota(jnp.int32, (own, slots), 0) == listed).astype(jnp.float32)
    pick = jnp.transpose(pick).astype(jnp.bfloat16)
    for load in loads:
        load.wait()

    def gather(head, carry):
        for i in range(3):
            fresh_out[head, :, pl.ds(i * HEAD_DIM, HEAD_DIM)] = jnp.dot(
                pick, fresh_own[i, :, columns(head)], preferred_element_type=jnp.float32
            ).astype(jnp.bfloat16)
        return carry

    lax.fori_loop(0, shards, gather, 0)

    def send_b(i, carry):
        to = peer(i)
        for src, dst, n in (
            (fresh_out.at[to], fresh_buf.at[me], 3),
            (list_out, list_buf.at[me], 4),
        ):
            pltpu.make_async_remote_copy(
                src_ref=src,
                dst_ref=dst,
                send_sem=send_sem.at[n],
                recv_sem=recv_sem.at[n],
                device_id={"seq": to},
                device_id_type=MESH,
            ).start()
        return carry

    lax.fori_loop(0, shards - 1, send_b, 0)
    pltpu.make_async_copy(fresh_out.at[me], fresh_buf.at[me], recv_sem.at[3]).start()
    pltpu.make_async_copy(list_out, list_buf.at[me], recv_sem.at[4]).start()

    v_buf[:, HEAD_DIM:] = jnp.ones((v_buf.shape[0], HEAD_DIM), jnp.bfloat16)

    def arrived(ref, n):
        pltpu.make_async_copy(ref, ref, recv_sem.at[n]).wait()

    arrived(k_buf, 0)
    arrived(v_buf.at[:, pl.ds(0, HEAD_DIM)], 1)
    arrived(q_buf, 2)

    def send_home(src, dst, to, n):
        @pl.when(to != me)
        def _():
            pltpu.make_async_remote_copy(
                src_ref=src,
                dst_ref=dst,
                send_sem=send_sem.at[n],
                recv_sem=recv_sem.at[n],
                device_id={"seq": to},
                device_id_type=MESH,
            ).start()

        @pl.when(to == me)
        def _():
            pltpu.make_async_copy(src, dst, recv_sem.at[n]).start()

    def refresh(i, carry):
        first = plane(i) * width
        block = pl.ds(pl.multiple_of(first * own, width * own), width * own)
        out = attend(q_buf[block, :], k_buf, v_buf)
        refresh_buf[block, :] = out.astype(jnp.bfloat16)
        for j in range(width):
            to = first + j
            send_home(refresh_buf.at[rows_of(to)], refresh_ref.at[:, columns(me)], to, 5)
        return carry

    lax.fori_loop(0, PLANES, refresh, 0)

    arrived(fresh_buf, 3)
    arrived(list_buf, 4)

    def update(i, carry):
        for j in range(width):
            shard = i * width + j
            at = list_buf[shard, 0:1, 0:slots]
            put = lax.broadcasted_iota(jnp.int32, (own, slots), 0) == at
            put = put.astype(jnp.float32)
            changed = jnp.max(put, axis=-1, keepdims=True) > 0.0
            new = jnp.dot(
                put.astype(jnp.bfloat16),
                fresh_buf[shard, :, HEAD_DIM:],
                preferred_element_type=jnp.float32,
            ).astype(jnp.bfloat16)
            block = rows_of(shard)
            k_buf[block, :] = jnp.where(changed, new[:, :HEAD_DIM], k_buf[block, :])
            v_buf[block, :HEAD_DIM] = jnp.where(
                changed, new[:, HEAD_DIM:], v_buf[block, :HEAD_DIM]
            )
        return carry

    lax.fori_loop(0, PLANES, update, 0)

    def cached(i, carry):
        firsts = [early_plane(2 * i + j) * width for j in range(2)]
        groups = [pl.ds(first, width) for first in firsts]
        query_block = jnp.concatenate([fresh_buf[g, :, 0:HEAD_DIM] for g in groups])
        out = attend(query_block.reshape(-1, HEAD_DIM), k_buf, v_buf)
        out = out.reshape(2, width, slots, HEAD_DIM)
        slot = lax.broadcasted_iota(jnp.int32, out.shape[1:], 1)
        for j, group in enumerate(groups):
            live = slot < list_buf[group, 0:1, HEAD_DIM - 1 :]
            cached_buf[group, :, :] = jnp.where(live, out[j], 0.0).astype(jnp.bfloat16)
        for first in firsts:
            for j in range(width):
                to = first + j
                send_home(cached_buf.at[to], cached_ref.at[:, columns(me)], to, 6)
        return carry

    lax.fori_loop(0, PLANES // 2, cached, 0)

    arrived(refresh_ref, 5)
    arrived(cached_ref, 6)

    def sent(ref, n):
        pltpu.make_async_copy(ref, ref, send_sem.at[n]).wait()

    others = pl.ds(0, (shards - 1) * own)
    for n in (0, 1, 2, 5):
        sent(q_buf.at[others, :], n)
    sent(fresh_buf.at[pl.ds(0, shards - 1)], 3)
    sent(list_buf.at[pl.ds(0, shards - 1)], 4)
    sent(cached_buf.at[pl.ds(0, shards - 1)], 6)


def hand_over(refresh_in, cached_in, refresh_ref, cached_ref, sem):
    copies = [
        pltpu.make_async_copy(refresh_in, refresh_ref, sem.at[0]),
        pltpu.make_async_copy(cached_in, cached_ref, sem.at[1]),
    ]
    for copy in copies:
        copy.start()
    for copy in copies:
        copy.wait()


def per_device(
    queries, keys, values, fresh_queries, fresh_keys, fresh_values, masked_rows, masked_counts
):
    own, width = queries.shape
    slots = masked_rows.shape[1]
    shards = lax.axis_size("seq")
    tokens = shards * own
    bf16 = jnp.bfloat16
    hbm = pl.BlockSpec(memory_space=pltpu.HBM)
    anywhere = pl.BlockSpec(memory_space=pl.ANY)
    results = pl.pallas_call(
        functools.partial(kernel, shards),
        name="attention",
        out_shape=(
            jax.ShapeDtypeStruct((own, width), bf16),
            jax.ShapeDtypeStruct((slots, width), bf16),
        ),
        in_specs=[hbm] * 6 + [pl.BlockSpec(memory_space=pltpu.SMEM)] * 2,
        out_specs=(anywhere, anywhere),
        scratch_shapes=[
            pltpu.VMEM((tokens, HEAD_DIM), bf16),
            pltpu.VMEM((tokens, HEAD_DIM), bf16),
            pltpu.VMEM((tokens, 2 * HEAD_DIM), bf16),
            pltpu.VMEM((3, own, width), bf16),
            pltpu.VMEM((shards, slots, 3 * HEAD_DIM), bf16),
            pltpu.VMEM((shards, slots, 3 * HEAD_DIM), bf16),
            pltpu.VMEM((1, HEAD_DIM), jnp.int32),
            pltpu.VMEM((shards, 1, HEAD_DIM), jnp.int32),
            pltpu.VMEM((tokens, HEAD_DIM), bf16),
            pltpu.VMEM((shards, slots, HEAD_DIM), bf16),
            pltpu.SemaphoreType.DMA((3,)),
            pltpu.SemaphoreType.DMA((7,)),
            pltpu.SemaphoreType.DMA((7,)),
        ],
        compiler_params=pltpu.CompilerParams(
            collective_id=0, has_side_effects=True, vmem_limit_bytes=VMEM_LIMIT
        ),
        cost_estimate=pl.CostEstimate(
            flops=6 * tokens * tokens * HEAD_DIM,
            bytes_accessed=12 * own * width,
            transcendentals=tokens * tokens * 3 // 2,
        ),
    )(
        queries,
        keys,
        values,
        fresh_queries,
        fresh_keys,
        fresh_values,
        masked_rows,
        masked_counts,
    )
    return pl.pallas_call(
        hand_over,
        name="hand_over",
        out_shape=tuple(jax.ShapeDtypeStruct(r.shape, r.dtype) for r in results),
        in_specs=[anywhere] * 2,
        out_specs=(hbm, hbm),
        scratch_shapes=[pltpu.SemaphoreType.DMA((2,))],
        compiler_params=pltpu.CompilerParams(vmem_limit_bytes=2**20),
    )(*results)


def solution(mesh):
    spread = P(("doc", "seq"), None)
    return jax.shard_map(
        per_device,
        mesh=mesh,
        in_specs=(spread,) * 7 + (P(("doc", "seq")),),
        out_specs=(spread, spread),
        check_vma=False,
    )
```

```python
import functools
import math

import jax
import jax.numpy as jnp
from jax import lax
from jax.experimental import pallas as pl
from jax.experimental.pallas import tpu as pltpu
from jax.sharding import PartitionSpec as P

HEAD_DIM = 128
PLANES = 8
VMEM_LIMIT = 105 * 2**19
MESH = pl.DeviceIdType.MESH
KEY_CHUNK = 256
EXP2_SCALE = math.log2(math.e) / math.sqrt(HEAD_DIM)


def attend(query_block, key_ref, value_ref):
    rows = query_block.shape[0]
    top = jnp.full((rows, 1), -jnp.inf, jnp.float32)
    total = jnp.zeros((rows, 2 * HEAD_DIM), jnp.float32)
    for c in range(0, key_ref.shape[0], KEY_CHUNK):
        scores = lax.dot_general(
            query_block,
            key_ref[pl.ds(c, KEY_CHUNK), :],
            (((1,), (1,)), ((), ())),
            preferred_element_type=jnp.float32,
        )
        new_top = jnp.maximum(top, jnp.max(scores, axis=-1, keepdims=True))
        powers = jnp.exp2((scores - new_top) * EXP2_SCALE).astype(jnp.bfloat16)
        total = total * jnp.exp2((top - new_top) * EXP2_SCALE) + jnp.dot(
            powers, value_ref[pl.ds(c, KEY_CHUNK), :], preferred_element_type=jnp.float32
        )
        top = new_top
    return total[:, :HEAD_DIM] / total[:, HEAD_DIM:]


def kernel(
    shards,
    q_ref,
    k_ref,
    v_ref,
    fq_ref,
    fk_ref,
    fv_ref,
    rows_ref,
    count_ref,
    refresh_ref,
    cached_ref,
    q_buf,
    k_buf,
    v_buf,
    fresh_own,
    fresh_out,
    fresh_buf,
    list_out,
    list_buf,
    refresh_buf,
    cached_buf,
    load_sem,
    ready_sem,
    send_sem,
    recv_sem,
):
    me = lax.axis_index("seq")
    width = shards // PLANES
    own = q_ref.shape[0]
    slots = rows_ref.shape[1]

    def plane(i):
        step = PLANES // 2 + lax.div(i + 1, 2) * (1 - 2 * lax.rem(i, 2))
        return lax.rem(lax.div(me, width) + step, PLANES)

    def peer(i):
        reach = PLANES - 1
        far = lax.div(i, reach) < width
        step = jnp.where(far, lax.div(i, reach) + 1, i - reach * width + 1)
        x = lax.rem(lax.rem(me, width) + step, width)
        return plane(jnp.where(far, lax.rem(i, reach), reach)) * width + x

    def early_plane(i):
        half = PLANES // 2
        turn = lax.rem(i, half)
        step = half // 2 + lax.div(turn + 1, 2) * (1 - 2 * lax.rem(turn, 2))
        return lax.div(i, half) * half + lax.rem(lax.rem(lax.div(me, width), half) + step, half)

    def columns(head):
        return pl.ds(pl.multiple_of(head * HEAD_DIM, HEAD_DIM), HEAD_DIM)

    def rows_of(shard):
        return pl.ds(pl.multiple_of(shard * own, own), own)

    def device(dz, dx):
        z = lax.rem(lax.div(me, width) + dz, PLANES)
        return z * width + lax.rem(lax.rem(me, width) + dx, width)

    def signal(sem, dz, dx):
        pl.semaphore_signal(
            sem, inc=1, device_id={"seq": device(dz, dx)}, device_id_type=MESH
        )

    plane_mates = [(0, dx) for dx in range(1, width)]
    column_far, column_near = [(2, 0), (PLANES - 2, 0)], [(1, 0), (PLANES - 1, 0)]
    barrier = pltpu.get_barrier_semaphore()
    for place in column_far + column_near + plane_mates:
        signal(barrier, *place)

    loads = [
        pltpu.make_async_copy(ref, fresh_own.at[i], load_sem.at[i])
        for i, ref in enumerate((fq_ref, fk_ref, fv_ref))
    ]
    for load in loads:
        load.start()

    stage_a = ((k_ref, k_buf, 0), (v_ref, v_buf, 1), (q_ref, q_buf, 2))

    def send_a(n, places, columns_on):
        ref, buf, _ = stage_a[n]

        def one(c, carry):
            for dz, dx in places:
                to = device(dz, dx + c)
                pltpu.make_async_remote_copy(
                    src_ref=ref.at[:, columns(to)],
                    dst_ref=buf.at[rows_of(me), pl.ds(0, HEAD_DIM)],
                    send_sem=send_sem.at[n],
                    recv_sem=recv_sem.at[n],
                    device_id={"seq": to},
                    device_id_type=MESH,
                ).start()
            return carry

        lax.fori_loop(*columns_on, one, 0)

    own_column, other_columns, all_columns = (0, 1), (1, width), (0, width)
    near = column_far + column_near
    far = [(PLANES // 2, 0), (PLANES // 2 - 1, 0), (PLANES // 2 + 1, 0)]

    pl.semaphore_wait(barrier, len(near) + len(plane_mates))
    for place in column_far + plane_mates:
        signal(ready_sem.at[0], *place)
    send_a(0, near, own_column)
    send_a(1, near, own_column)
    pl.semaphore_wait(ready_sem.at[0], len(column_far) + len(plane_mates))
    for place in plane_mates:
        signal(ready_sem.at[1], *place)
    send_a(0, far, own_column)
    send_a(0, near, other_columns)
    pl.semaphore_wait(ready_sem.at[1], len(plane_mates))
    send_a(0, far, other_columns)
    send_a(1, far, own_column)
    send_a(1, far + near, other_columns)
    send_a(2, far + near, all_columns)
    for n in range(3):
        send_a(n, [(0, 0)], other_columns)
    for ref, buf, n in stage_a:
        pltpu.make_async_copy(
            ref.at[:, columns(me)], buf.at[rows_of(me), pl.ds(0, HEAD_DIM)], recv_sem.at[n]
        ).start()

    count = count_ref[0]
    lane = lax.broadcasted_iota(jnp.int32, (1, slots), 1)
    listed = jnp.zeros((1, slots), jnp.int32)
    for j in range(slots):
        listed = jnp.where(lane == j, rows_ref[0, j], listed)
    list_out[...] = jnp.full(list_out.shape, count, jnp.int32)
    list_out[0:1, 0:slots] = jnp.where(lane < count, listed, -1)
    pick = (lax.broadcasted_iota(jnp.int32, (own, slots), 0) == listed).astype(jnp.float32)
    pick = jnp.transpose(pick).astype(jnp.bfloat16)
    for load in loads:
        load.wait()

    def gather(head, carry):
        for i in range(3):
            fresh_out[head, :, pl.ds(i * HEAD_DIM, HEAD_DIM)] = jnp.dot(
                pick, fresh_own[i, :, columns(head)], preferred_element_type=jnp.float32
            ).astype(jnp.bfloat16)
        return carry

    lax.fori_loop(0, shards, gather, 0)

    def send_b(i, carry):
        to = peer(i)
        for src, dst, n in (
            (fresh_out.at[to], fresh_buf.at[me], 3),
            (list_out, list_buf.at[me], 4),
        ):
            pltpu.make_async_remote_copy(
                src_ref=src,
                dst_ref=dst,
                send_sem=send_sem.at[n],
                recv_sem=recv_sem.at[n],
                device_id={"seq": to},
                device_id_type=MESH,
            ).start()
        return carry

    lax.fori_loop(0, shards - 1, send_b, 0)
    pltpu.make_async_copy(fresh_out.at[me], fresh_buf.at[me], recv_sem.at[3]).start()
    pltpu.make_async_copy(list_out, list_buf.at[me], recv_sem.at[4]).start()

    v_buf[:, HEAD_DIM:] = jnp.ones((v_buf.shape[0], HEAD_DIM), jnp.bfloat16)

    def arrived(ref, n):
        pltpu.make_async_copy(ref, ref, recv_sem.at[n]).wait()

    arrived(k_buf, 0)
    arrived(v_buf.at[:, pl.ds(0, HEAD_DIM)], 1)
    arrived(q_buf, 2)

    def send_home(src, dst, to, n):
        @pl.when(to != me)
        def _():
            pltpu.make_async_remote_copy(
                src_ref=src,
                dst_ref=dst,
                send_sem=send_sem.at[n],
                recv_sem=recv_sem.at[n],
                device_id={"seq": to},
                device_id_type=MESH,
            ).start()

        @pl.when(to == me)
        def _():
            pltpu.make_async_copy(src, dst, recv_sem.at[n]).start()

    def refresh(i, carry):
        first = plane(i) * width
        block = pl.ds(pl.multiple_of(first * own, width * own), width * own)
        out = attend(q_buf[block, :], k_buf, v_buf)
        refresh_buf[block, :] = out.astype(jnp.bfloat16)
        for j in range(width):
            to = first + j
            send_home(refresh_buf.at[rows_of(to)], refresh_ref.at[:, columns(me)], to, 5)
        return carry

    lax.fori_loop(0, PLANES, refresh, 0)

    arrived(fresh_buf, 3)
    arrived(list_buf, 4)

    def update(i, carry):
        for j in range(width):
            shard = i * width + j
            at = list_buf[shard, 0:1, 0:slots]
            put = lax.broadcasted_iota(jnp.int32, (own, slots), 0) == at
            put = put.astype(jnp.float32)
            changed = jnp.max(put, axis=-1, keepdims=True) > 0.0
            new = jnp.dot(
                put.astype(jnp.bfloat16),
                fresh_buf[shard, :, HEAD_DIM:],
                preferred_element_type=jnp.float32,
            ).astype(jnp.bfloat16)
            block = rows_of(shard)
            k_buf[block, :] = jnp.where(changed, new[:, :HEAD_DIM], k_buf[block, :])
            v_buf[block, :HEAD_DIM] = jnp.where(
                changed, new[:, HEAD_DIM:], v_buf[block, :HEAD_DIM]
            )
        return carry

    lax.fori_loop(0, PLANES, update, 0)

    def cached(i, carry):
        firsts = [early_plane(2 * i + j) * width for j in range(2)]
        groups = [pl.ds(first, width) for first in firsts]
        query_block = jnp.concatenate([fresh_buf[g, :, 0:HEAD_DIM] for g in groups])
        out = attend(query_block.reshape(-1, HEAD_DIM), k_buf, v_buf)
        out = out.reshape(2, width, slots, HEAD_DIM)
        slot = lax.broadcasted_iota(jnp.int32, out.shape[1:], 1)
        for j, group in enumerate(groups):
            live = slot < list_buf[group, 0:1, HEAD_DIM - 1 :]
            cached_buf[group, :, :] = jnp.where(live, out[j], 0.0).astype(jnp.bfloat16)
        for first in firsts:
            for j in range(width):
                to = first + j
                send_home(cached_buf.at[to], cached_ref.at[:, columns(me)], to, 6)
        return carry

    lax.fori_loop(0, PLANES // 2, cached, 0)

    arrived(refresh_ref, 5)
    arrived(cached_ref, 6)

    def sent(ref, n):
        pltpu.make_async_copy(ref, ref, send_sem.at[n]).wait()

    others = pl.ds(0, (shards - 1) * own)
    for n in (0, 1, 2, 5):
        sent(q_buf.at[others, :], n)
    sent(fresh_buf.at[pl.ds(0, shards - 1)], 3)
    sent(list_buf.at[pl.ds(0, shards - 1)], 4)
    sent(cached_buf.at[pl.ds(0, shards - 1)], 6)


def hand_over(refresh_in, cached_in, refresh_ref, cached_ref, sem):
    copies = [
        pltpu.make_async_copy(refresh_in, refresh_ref, sem.at[0]),
        pltpu.make_async_copy(cached_in, cached_ref, sem.at[1]),
    ]
    for copy in copies:
        copy.start()
    for copy in copies:
        copy.wait()


def per_device(
    queries, keys, values, fresh_queries, fresh_keys, fresh_values, masked_rows, masked_counts
):
    own, width = queries.shape
    slots = masked_rows.shape[1]
    shards = lax.axis_size("seq")
    tokens = shards * own
    bf16 = jnp.bfloat16
    hbm = pl.BlockSpec(memory_space=pltpu.HBM)
    anywhere = pl.BlockSpec(memory_space=pl.ANY)
    results = pl.pallas_call(
        functools.partial(kernel, shards),
        name="attention",
        out_shape=(
            jax.ShapeDtypeStruct((own, width), bf16),
            jax.ShapeDtypeStruct((slots, width), bf16),
        ),
        in_specs=[hbm] * 6 + [pl.BlockSpec(memory_space=pltpu.SMEM)] * 2,
        out_specs=(anywhere, anywhere),
        scratch_shapes=[
            pltpu.VMEM((tokens, HEAD_DIM), bf16),
            pltpu.VMEM((tokens, HEAD_DIM), bf16),
            pltpu.VMEM((tokens, 2 * HEAD_DIM), bf16),
            pltpu.VMEM((3, own, width), bf16),
            pltpu.VMEM((shards, slots, 3 * HEAD_DIM), bf16),
            pltpu.VMEM((shards, slots, 3 * HEAD_DIM), bf16),
            pltpu.VMEM((1, HEAD_DIM), jnp.int32),
            pltpu.VMEM((shards, 1, HEAD_DIM), jnp.int32),
            pltpu.VMEM((tokens, HEAD_DIM), bf16),
            pltpu.VMEM((shards, slots, HEAD_DIM), bf16),
            pltpu.SemaphoreType.DMA((3,)),
            pltpu.SemaphoreType.REGULAR((2,)),
            pltpu.SemaphoreType.DMA((7,)),
            pltpu.SemaphoreType.DMA((7,)),
        ],
        compiler_params=pltpu.CompilerParams(
            collective_id=0, has_side_effects=True, vmem_limit_bytes=VMEM_LIMIT
        ),
        cost_estimate=pl.CostEstimate(
            flops=6 * tokens * tokens * HEAD_DIM,
            bytes_accessed=12 * own * width,
            transcendentals=tokens * tokens * 3 // 2,
        ),
    )(
        queries,
        keys,
        values,
        fresh_queries,
        fresh_keys,
        fresh_values,
        masked_rows,
        masked_counts,
    )
    return pl.pallas_call(
        hand_over,
        name="hand_over",
        out_shape=tuple(jax.ShapeDtypeStruct(r.shape, r.dtype) for r in results),
        in_specs=[anywhere] * 2,
        out_specs=(hbm, hbm),
        scratch_shapes=[pltpu.SemaphoreType.DMA((2,))],
        compiler_params=pltpu.CompilerParams(vmem_limit_bytes=2**20),
    )(*results)


def solution(mesh):
    spread = P(("doc", "seq"), None)
    return jax.shard_map(
        per_device,
        mesh=mesh,
        in_specs=(spread,) * 7 + (P(("doc", "seq")),),
        out_specs=(spread, spread),
        check_vma=False,
    )
```

```python
import functools
import math

import jax
import jax.numpy as jnp
from jax import lax
from jax.experimental import pallas as pl
from jax.experimental.pallas import tpu as pltpu
from jax.sharding import PartitionSpec as P

HEAD_DIM = 128
PLANES = 8
VMEM_LIMIT = 40 * 2**20
MESH = pl.DeviceIdType.MESH
KEY_CHUNK = 256
EXP2_SCALE = math.log2(math.e) / math.sqrt(HEAD_DIM)


def attend(query_block, key_ref, value_ref):
    rows = query_block.shape[0]
    top = jnp.full((rows, 1), -jnp.inf, jnp.float32)
    total = jnp.zeros((rows, 2 * HEAD_DIM), jnp.float32)
    for c in range(0, key_ref.shape[0], KEY_CHUNK):
        scores = lax.dot_general(
            query_block,
            key_ref[pl.ds(c, KEY_CHUNK), :],
            (((1,), (1,)), ((), ())),
            preferred_element_type=jnp.float32,
        )
        new_top = jnp.maximum(top, jnp.max(scores, axis=-1, keepdims=True))
        powers = jnp.exp2((scores - new_top) * EXP2_SCALE).astype(jnp.bfloat16)
        total = total * jnp.exp2((top - new_top) * EXP2_SCALE) + jnp.dot(
            powers, value_ref[pl.ds(c, KEY_CHUNK), :], preferred_element_type=jnp.float32
        )
        top = new_top
    return total[:, :HEAD_DIM] / total[:, HEAD_DIM:]


def kernel(
    shards,
    q_ref,
    k_ref,
    v_ref,
    fq_ref,
    fk_ref,
    fv_ref,
    rows_ref,
    count_ref,
    refresh_ref,
    cached_ref,
    q_buf,
    k_buf,
    v_buf,
    rows_own,
    fresh_own,
    fresh_out,
    fresh_buf,
    list_out,
    list_buf,
    refresh_buf,
    cached_buf,
    load_sem,
    ready_sem,
    send_sem,
    recv_sem,
):
    me = lax.axis_index("seq")
    width = shards // PLANES
    own = q_ref.shape[0]
    slots = rows_ref.shape[1]

    def plane(i):
        step = PLANES // 2 + lax.div(i + 1, 2) * (1 - 2 * lax.rem(i, 2))
        return lax.rem(lax.div(me, width) + step, PLANES)

    def peer(i):
        reach = PLANES - 1
        far = lax.div(i, reach) < width
        step = jnp.where(far, lax.div(i, reach) + 1, i - reach * width + 1)
        x = lax.rem(lax.rem(me, width) + step, width)
        return plane(jnp.where(far, lax.rem(i, reach), reach)) * width + x

    def early_plane(i):
        half = PLANES // 2
        turn = lax.rem(i, half)
        step = half // 2 + lax.div(turn + 1, 2) * (1 - 2 * lax.rem(turn, 2))
        return lax.div(i, half) * half + lax.rem(lax.rem(lax.div(me, width), half) + step, half)

    def columns(head):
        return pl.ds(pl.multiple_of(head * HEAD_DIM, HEAD_DIM), HEAD_DIM)

    def rows_of(shard):
        return pl.ds(pl.multiple_of(shard * own, own), own)

    def device(dz, dx):
        z = lax.rem(lax.div(me, width) + dz, PLANES)
        return z * width + lax.rem(lax.rem(me, width) + dx, width)

    def signal(sem, dz, dx):
        pl.semaphore_signal(
            sem, inc=1, device_id={"seq": device(dz, dx)}, device_id_type=MESH
        )

    plane_mates = [(0, dx) for dx in range(1, width)]
    column_far, column_near = [(2, 0), (PLANES - 2, 0)], [(1, 0), (PLANES - 1, 0)]
    barrier = pltpu.get_barrier_semaphore()
    for place in column_far + column_near + plane_mates:
        signal(barrier, *place)

    loads = [
        pltpu.make_async_copy(ref, fresh_own.at[i], load_sem.at[i])
        for i, ref in enumerate((fq_ref, fk_ref, fv_ref))
    ]
    loads.append(pltpu.make_async_copy(rows_ref, rows_own, load_sem.at[3]))
    for load in loads:
        load.start()

    stage_a = ((k_ref, k_buf, 0), (v_ref, v_buf, 1), (q_ref, q_buf, 2))

    def send_a(n, places, columns_on):
        ref, buf, _ = stage_a[n]

        def one(c, carry):
            for dz, dx in places:
                to = device(dz, dx + c)
                pltpu.make_async_remote_copy(
                    src_ref=ref.at[:, columns(to)],
                    dst_ref=buf.at[rows_of(me), pl.ds(0, HEAD_DIM)],
                    send_sem=send_sem.at[n],
                    recv_sem=recv_sem.at[n],
                    device_id={"seq": to},
                    device_id_type=MESH,
                ).start()
            return carry

        lax.fori_loop(*columns_on, one, 0)

    own_column, other_columns, all_columns = (0, 1), (1, width), (0, width)
    near = column_far + column_near
    far = [(PLANES // 2, 0), (PLANES // 2 - 1, 0), (PLANES // 2 + 1, 0)]

    pl.semaphore_wait(barrier, len(near) + len(plane_mates))
    for place in column_far + plane_mates:
        signal(ready_sem.at[0], *place)
    send_a(0, near, own_column)
    send_a(1, near, own_column)
    pl.semaphore_wait(ready_sem.at[0], len(column_far) + len(plane_mates))
    for place in plane_mates:
        signal(ready_sem.at[1], *place)
    send_a(0, far, own_column)
    send_a(0, near, other_columns)
    pl.semaphore_wait(ready_sem.at[1], len(plane_mates))
    send_a(0, far, other_columns)
    send_a(1, far, own_column)
    send_a(1, far + near, other_columns)
    send_a(2, far + near, all_columns)
    for n in range(3):
        send_a(n, [(0, 0)], other_columns)
    for ref, buf, n in stage_a:
        pltpu.make_async_copy(
            ref.at[:, columns(me)], buf.at[rows_of(me), pl.ds(0, HEAD_DIM)], recv_sem.at[n]
        ).start()

    for load in loads:
        load.wait()
    count = count_ref[0]
    lane = lax.broadcasted_iota(jnp.int32, (1, slots), 1)
    listed = rows_own[...]
    list_out[...] = jnp.full(list_out.shape, count, jnp.int32)
    list_out[0:1, 0:slots] = jnp.where(lane < count, listed, -1)
    pick = (lax.broadcasted_iota(jnp.int32, (own, slots), 0) == listed).astype(jnp.float32)
    pick = jnp.transpose(pick).astype(jnp.bfloat16)

    def gather(head, carry):
        for i in range(3):
            fresh_out[head, :, pl.ds(i * HEAD_DIM, HEAD_DIM)] = jnp.dot(
                pick, fresh_own[i, :, columns(head)], preferred_element_type=jnp.float32
            ).astype(jnp.bfloat16)
        return carry

    lax.fori_loop(0, shards, gather, 0)

    def send_b(i, carry):
        to = peer(i)
        for src, dst, n in (
            (fresh_out.at[to], fresh_buf.at[me], 3),
            (list_out, list_buf.at[me], 4),
        ):
            pltpu.make_async_remote_copy(
                src_ref=src,
                dst_ref=dst,
                send_sem=send_sem.at[n],
                recv_sem=recv_sem.at[n],
                device_id={"seq": to},
                device_id_type=MESH,
            ).start()
        return carry

    lax.fori_loop(0, shards - 1, send_b, 0)
    pltpu.make_async_copy(fresh_out.at[me], fresh_buf.at[me], recv_sem.at[3]).start()
    pltpu.make_async_copy(list_out, list_buf.at[me], recv_sem.at[4]).start()

    v_buf[:, HEAD_DIM:] = jnp.ones((v_buf.shape[0], HEAD_DIM), jnp.bfloat16)

    def arrived(ref, n):
        pltpu.make_async_copy(ref, ref, recv_sem.at[n]).wait()

    arrived(k_buf, 0)
    arrived(v_buf.at[:, pl.ds(0, HEAD_DIM)], 1)
    arrived(q_buf, 2)

    def send_home(src, dst, to, n):
        @pl.when(to != me)
        def _():
            pltpu.make_async_remote_copy(
                src_ref=src,
                dst_ref=dst,
                send_sem=send_sem.at[n],
                recv_sem=recv_sem.at[n],
                device_id={"seq": to},
                device_id_type=MESH,
            ).start()

        @pl.when(to == me)
        def _():
            pltpu.make_async_copy(src, dst, recv_sem.at[n]).start()

    eager = lax.rem(lax.axis_index("doc"), 2) == 0

    def send_refresh(first):
        for j in range(width):
            to = first + j
            send_home(refresh_buf.at[rows_of(to)], refresh_ref.at[:, columns(me)], to, 5)

    def refresh(i, carry):
        first = plane(i) * width
        block = pl.ds(pl.multiple_of(first * own, width * own), width * own)
        out = attend(q_buf[block, :], k_buf, v_buf)
        refresh_buf[block, :] = out.astype(jnp.bfloat16)

        @pl.when(eager)
        def _():
            send_refresh(first)

        return carry

    lax.fori_loop(0, PLANES, refresh, 0)

    @pl.when(jnp.logical_not(eager))
    def _():
        def late(i, carry):
            send_refresh(plane(i) * width)
            return carry

        lax.fori_loop(0, PLANES, late, 0)


    arrived(fresh_buf, 3)
    arrived(list_buf, 4)

    def update(i, carry):
        for j in range(width):
            shard = i * width + j
            at = list_buf[shard, 0:1, 0:slots]
            put = lax.broadcasted_iota(jnp.int32, (own, slots), 0) == at
            put = put.astype(jnp.float32)
            changed = jnp.max(put, axis=-1, keepdims=True) > 0.0
            new = jnp.dot(
                put.astype(jnp.bfloat16),
                fresh_buf[shard, :, HEAD_DIM:],
                preferred_element_type=jnp.float32,
            ).astype(jnp.bfloat16)
            block = rows_of(shard)
            k_buf[block, :] = jnp.where(changed, new[:, :HEAD_DIM], k_buf[block, :])
            v_buf[block, :HEAD_DIM] = jnp.where(
                changed, new[:, HEAD_DIM:], v_buf[block, :HEAD_DIM]
            )
        return carry

    lax.fori_loop(0, PLANES, update, 0)

    def cached(i, carry):
        firsts = [early_plane(2 * i + j) * width for j in range(2)]
        groups = [pl.ds(first, width) for first in firsts]
        query_block = jnp.concatenate([fresh_buf[g, :, 0:HEAD_DIM] for g in groups])
        out = attend(query_block.reshape(-1, HEAD_DIM), k_buf, v_buf)
        out = out.reshape(2, width, slots, HEAD_DIM)
        slot = lax.broadcasted_iota(jnp.int32, out.shape[1:], 1)
        for j, group in enumerate(groups):
            live = slot < list_buf[group, 0:1, HEAD_DIM - 1 :]
            cached_buf[group, :, :] = jnp.where(live, out[j], 0.0).astype(jnp.bfloat16)
        for first in firsts:
            for j in range(width):
                to = first + j
                send_home(cached_buf.at[to], cached_ref.at[:, columns(me)], to, 6)
        return carry

    lax.fori_loop(0, PLANES // 2, cached, 0)

    arrived(refresh_ref, 5)
    arrived(cached_ref, 6)

    def sent(ref, n):
        pltpu.make_async_copy(ref, ref, send_sem.at[n]).wait()

    others = pl.ds(0, (shards - 1) * own)
    for n in (0, 1, 2, 5):
        sent(q_buf.at[others, :], n)
    sent(fresh_buf.at[pl.ds(0, shards - 1)], 3)
    sent(list_buf.at[pl.ds(0, shards - 1)], 4)
    sent(cached_buf.at[pl.ds(0, shards - 1)], 6)


def hand_over(refresh_in, cached_in, refresh_ref, cached_ref, sem):
    copies = [
        pltpu.make_async_copy(refresh_in, refresh_ref, sem.at[0]),
        pltpu.make_async_copy(cached_in, cached_ref, sem.at[1]),
    ]
    for copy in copies:
        copy.start()
    for copy in copies:
        copy.wait()


def per_device(
    queries, keys, values, fresh_queries, fresh_keys, fresh_values, masked_rows, masked_counts
):
    own, width = queries.shape
    slots = masked_rows.shape[1]
    shards = lax.axis_size("seq")
    tokens = shards * own
    bf16 = jnp.bfloat16
    hbm = pl.BlockSpec(memory_space=pltpu.HBM)
    anywhere = pl.BlockSpec(memory_space=pl.ANY)
    operands = [
        pltpu.with_memory_space_constraint(operand, pltpu.HBM)
        for operand in (
            queries,
            keys,
            values,
            fresh_queries,
            fresh_keys,
            fresh_values,
            masked_rows,
        )
    ]
    results = pl.pallas_call(
        functools.partial(kernel, shards),
        name="attention",
        out_shape=(
            jax.ShapeDtypeStruct((own, width), bf16),
            jax.ShapeDtypeStruct((slots, width), bf16),
        ),
        in_specs=[hbm] * 7 + [pl.BlockSpec(memory_space=pltpu.SMEM)],
        out_specs=(anywhere, anywhere),
        scratch_shapes=[
            pltpu.VMEM((tokens, HEAD_DIM), bf16),
            pltpu.VMEM((tokens, HEAD_DIM), bf16),
            pltpu.VMEM((tokens, 2 * HEAD_DIM), bf16),
            pltpu.VMEM((1, slots), jnp.int32),
            pltpu.VMEM((3, own, width), bf16),
            pltpu.VMEM((shards, slots, 3 * HEAD_DIM), bf16),
            pltpu.VMEM((shards, slots, 3 * HEAD_DIM), bf16),
            pltpu.VMEM((1, HEAD_DIM), jnp.int32),
            pltpu.VMEM((shards, 1, HEAD_DIM), jnp.int32),
            pltpu.VMEM((tokens, HEAD_DIM), bf16),
            pltpu.VMEM((shards, slots, HEAD_DIM), bf16),
            pltpu.SemaphoreType.DMA((4,)),
            pltpu.SemaphoreType.REGULAR((2,)),
            pltpu.SemaphoreType.DMA((7,)),
            pltpu.SemaphoreType.DMA((7,)),
        ],
        compiler_params=pltpu.CompilerParams(
            collective_id=0, has_side_effects=True, vmem_limit_bytes=VMEM_LIMIT
        ),
        cost_estimate=pl.CostEstimate(
            flops=6 * tokens * tokens * HEAD_DIM,
            bytes_accessed=12 * own * width,
            transcendentals=tokens * tokens * 3 // 2,
        ),
    )(
        *operands,
        masked_counts,
    )
    return pl.pallas_call(
        hand_over,
        name="hand_over",
        out_shape=tuple(jax.ShapeDtypeStruct(r.shape, r.dtype) for r in results),
        in_specs=[anywhere] * 2,
        out_specs=(hbm, hbm),
        scratch_shapes=[pltpu.SemaphoreType.DMA((2,))],
        compiler_params=pltpu.CompilerParams(vmem_limit_bytes=2**20),
    )(*results)


def solution(mesh):
    spread = P(("doc", "seq"), None)
    return jax.shard_map(
        per_device,
        mesh=mesh,
        in_specs=(spread,) * 7 + (P(("doc", "seq")),),
        out_specs=(spread, spread),
        check_vma=False,
    )
```

```python
import functools
import math

import jax
import jax.numpy as jnp
from jax import lax
from jax.experimental import pallas as pl
from jax.experimental.pallas import tpu as pltpu
from jax.sharding import PartitionSpec as P

HEAD_DIM = 128
PLANES = 8
VMEM_LIMIT = 40 * 2**20
MESH = pl.DeviceIdType.MESH
KEY_CHUNK = 256
EXP2_SCALE = math.log2(math.e) / math.sqrt(HEAD_DIM)


def attend(query_block, key_ref, value_ref):
    rows = query_block.shape[0]
    top = jnp.full((rows, 1), -jnp.inf, jnp.float32)
    total = jnp.zeros((rows, 2 * HEAD_DIM), jnp.float32)
    for c in range(0, key_ref.shape[0], KEY_CHUNK):
        scores = lax.dot_general(
            query_block,
            key_ref[pl.ds(c, KEY_CHUNK), :],
            (((1,), (1,)), ((), ())),
            preferred_element_type=jnp.float32,
        )
        new_top = jnp.maximum(top, jnp.max(scores, axis=-1, keepdims=True))
        powers = jnp.exp2((scores - new_top) * EXP2_SCALE).astype(jnp.bfloat16)
        total = total * jnp.exp2((top - new_top) * EXP2_SCALE) + jnp.dot(
            powers, value_ref[pl.ds(c, KEY_CHUNK), :], preferred_element_type=jnp.float32
        )
        top = new_top
    return total[:, :HEAD_DIM] / total[:, HEAD_DIM:]


def kernel(
    shards,
    q_ref,
    k_ref,
    v_ref,
    fq_ref,
    fk_ref,
    fv_ref,
    rows_ref,
    count_ref,
    refresh_ref,
    cached_ref,
    q_buf,
    k_buf,
    v_buf,
    rows_own,
    fresh_own,
    fresh_out,
    fresh_buf,
    list_out,
    list_buf,
    refresh_buf,
    cached_buf,
    load_sem,
    ready_sem,
    send_sem,
    recv_sem,
):
    me = lax.axis_index("seq")
    width = shards // PLANES
    own = q_ref.shape[0]
    slots = rows_ref.shape[1]

    def plane(i):
        step = PLANES // 2 + lax.div(i + 1, 2) * (1 - 2 * lax.rem(i, 2))
        return lax.rem(lax.div(me, width) + step, PLANES)

    def peer(i):
        reach = PLANES - 1
        far = lax.div(i, reach) < width
        step = jnp.where(far, lax.div(i, reach) + 1, i - reach * width + 1)
        x = lax.rem(lax.rem(me, width) + step, width)
        return plane(jnp.where(far, lax.rem(i, reach), reach)) * width + x

    def early_plane(i):
        half = PLANES // 2
        turn = lax.rem(i, half)
        step = half // 2 + lax.div(turn + 1, 2) * (1 - 2 * lax.rem(turn, 2))
        return lax.div(i, half) * half + lax.rem(lax.rem(lax.div(me, width), half) + step, half)

    def columns(head):
        return pl.ds(pl.multiple_of(head * HEAD_DIM, HEAD_DIM), HEAD_DIM)

    def rows_of(shard):
        return pl.ds(pl.multiple_of(shard * own, own), own)

    def device(dz, dx):
        z = lax.rem(lax.div(me, width) + dz, PLANES)
        return z * width + lax.rem(lax.rem(me, width) + dx, width)

    def signal(sem, dz, dx):
        pl.semaphore_signal(
            sem, inc=1, device_id={"seq": device(dz, dx)}, device_id_type=MESH
        )

    plane_mates = [(0, dx) for dx in range(1, width)]
    column_far, column_near = [(2, 0), (PLANES - 2, 0)], [(1, 0), (PLANES - 1, 0)]
    barrier = pltpu.get_barrier_semaphore()
    for place in column_far + column_near + plane_mates:
        signal(barrier, *place)

    loads = [
        pltpu.make_async_copy(ref, fresh_own.at[i], load_sem.at[i])
        for i, ref in enumerate((fq_ref, fk_ref, fv_ref))
    ]
    loads.append(pltpu.make_async_copy(rows_ref, rows_own, load_sem.at[3]))
    for load in loads:
        load.start()

    stage_a = ((k_ref, k_buf, 0), (v_ref, v_buf, 1), (q_ref, q_buf, 2))

    def send_a(n, places, columns_on):
        ref, buf, _ = stage_a[n]

        def one(c, carry):
            for dz, dx in places:
                to = device(dz, dx + c)
                pltpu.make_async_remote_copy(
                    src_ref=ref.at[:, columns(to)],
                    dst_ref=buf.at[rows_of(me), pl.ds(0, HEAD_DIM)],
                    send_sem=send_sem.at[n],
                    recv_sem=recv_sem.at[n],
                    device_id={"seq": to},
                    device_id_type=MESH,
                ).start()
            return carry

        lax.fori_loop(*columns_on, one, 0)

    own_column, other_columns, all_columns = (0, 1), (1, width), (0, width)
    near = column_far + column_near
    far = [(PLANES // 2, 0), (PLANES // 2 - 1, 0), (PLANES // 2 + 1, 0)]

    pl.semaphore_wait(barrier, len(near) + len(plane_mates))
    for place in column_far + plane_mates:
        signal(ready_sem.at[0], *place)
    send_a(0, near, own_column)
    send_a(1, near, own_column)
    pl.semaphore_wait(ready_sem.at[0], len(column_far) + len(plane_mates))
    for place in plane_mates:
        signal(ready_sem.at[1], *place)
    send_a(0, far, own_column)
    send_a(0, near, other_columns)
    pl.semaphore_wait(ready_sem.at[1], len(plane_mates))
    send_a(0, far, other_columns)
    send_a(1, far, own_column)
    send_a(1, far + near, other_columns)
    send_a(2, far + near, all_columns)
    for n in range(3):
        send_a(n, [(0, 0)], other_columns)
    for ref, buf, n in stage_a:
        pltpu.make_async_copy(
            ref.at[:, columns(me)], buf.at[rows_of(me), pl.ds(0, HEAD_DIM)], recv_sem.at[n]
        ).start()

    for load in loads:
        load.wait()
    count = count_ref[0]
    lane = lax.broadcasted_iota(jnp.int32, (1, slots), 1)
    listed = rows_own[...]
    list_out[...] = jnp.full(list_out.shape, count, jnp.int32)
    list_out[0:1, 0:slots] = jnp.where(lane < count, listed, -1)
    pick = (lax.broadcasted_iota(jnp.int32, (own, slots), 0) == listed).astype(jnp.float32)
    pick = jnp.transpose(pick).astype(jnp.bfloat16)

    def gather(head, carry):
        for i in range(3):
            fresh_out[head, :, pl.ds(i * HEAD_DIM, HEAD_DIM)] = jnp.dot(
                pick, fresh_own[i, :, columns(head)], preferred_element_type=jnp.float32
            ).astype(jnp.bfloat16)
        return carry

    lax.fori_loop(0, shards, gather, 0)

    def send_b(i, carry):
        to = peer(i)
        for src, dst, n in (
            (fresh_out.at[to], fresh_buf.at[me], 3),
            (list_out, list_buf.at[me], 4),
        ):
            pltpu.make_async_remote_copy(
                src_ref=src,
                dst_ref=dst,
                send_sem=send_sem.at[n],
                recv_sem=recv_sem.at[n],
                device_id={"seq": to},
                device_id_type=MESH,
            ).start()
        return carry

    lax.fori_loop(0, shards - 1, send_b, 0)
    pltpu.make_async_copy(fresh_out.at[me], fresh_buf.at[me], recv_sem.at[3]).start()
    pltpu.make_async_copy(list_out, list_buf.at[me], recv_sem.at[4]).start()

    v_buf[:, HEAD_DIM:] = jnp.ones((v_buf.shape[0], HEAD_DIM), jnp.bfloat16)

    def arrived(ref, n):
        pltpu.make_async_copy(ref, ref, recv_sem.at[n]).wait()

    arrived(k_buf, 0)
    arrived(v_buf.at[:, pl.ds(0, HEAD_DIM)], 1)
    arrived(q_buf, 2)

    def send_home(src, dst, to, n):
        @pl.when(to != me)
        def _():
            pltpu.make_async_remote_copy(
                src_ref=src,
                dst_ref=dst,
                send_sem=send_sem.at[n],
                recv_sem=recv_sem.at[n],
                device_id={"seq": to},
                device_id_type=MESH,
            ).start()

        @pl.when(to == me)
        def _():
            pltpu.make_async_copy(src, dst, recv_sem.at[n]).start()

    eager = lax.rem(lax.axis_index("doc"), 2) == 0

    def send_refresh(first):
        for j in range(width):
            to = first + j
            send_home(refresh_buf.at[rows_of(to)], refresh_ref.at[:, columns(me)], to, 5)

    def refresh(i, carry):
        first = plane(i) * width
        block = pl.ds(pl.multiple_of(first * own, width * own), width * own)
        out = attend(q_buf[block, :], k_buf, v_buf)
        refresh_buf[block, :] = out.astype(jnp.bfloat16)

        @pl.when(eager)
        def _():
            send_refresh(first)

        return carry

    lax.fori_loop(0, PLANES, refresh, 0)

    def send_late(begin, end):
        @pl.when(jnp.logical_not(eager))
        def _():
            def late(i, carry):
                send_refresh(plane(i) * width)
                return carry

            lax.fori_loop(begin, end, late, 0)

    send_late(0, 1)


    arrived(fresh_buf, 3)
    arrived(list_buf, 4)
    send_late(1, PLANES)

    def update(i, carry):
        for j in range(width):
            shard = i * width + j
            at = list_buf[shard, 0:1, 0:slots]
            put = lax.broadcasted_iota(jnp.int32, (own, slots), 0) == at
            put = put.astype(jnp.float32)
            changed = jnp.max(put, axis=-1, keepdims=True) > 0.0
            new = jnp.dot(
                put.astype(jnp.bfloat16),
                fresh_buf[shard, :, HEAD_DIM:],
                preferred_element_type=jnp.float32,
            ).astype(jnp.bfloat16)
            block = rows_of(shard)
            k_buf[block, :] = jnp.where(changed, new[:, :HEAD_DIM], k_buf[block, :])
            v_buf[block, :HEAD_DIM] = jnp.where(
                changed, new[:, HEAD_DIM:], v_buf[block, :HEAD_DIM]
            )
        return carry

    lax.fori_loop(0, PLANES, update, 0)

    def cached(i, carry):
        firsts = [early_plane(2 * i + j) * width for j in range(2)]
        groups = [pl.ds(first, width) for first in firsts]
        query_block = jnp.concatenate([fresh_buf[g, :, 0:HEAD_DIM] for g in groups])
        out = attend(query_block.reshape(-1, HEAD_DIM), k_buf, v_buf)
        out = out.reshape(2, width, slots, HEAD_DIM)
        slot = lax.broadcasted_iota(jnp.int32, out.shape[1:], 1)
        for j, group in enumerate(groups):
            live = slot < list_buf[group, 0:1, HEAD_DIM - 1 :]
            cached_buf[group, :, :] = jnp.where(live, out[j], 0.0).astype(jnp.bfloat16)
        for first in firsts:
            for j in range(width):
                to = first + j
                send_home(cached_buf.at[to], cached_ref.at[:, columns(me)], to, 6)
        return carry

    lax.fori_loop(0, PLANES // 2, cached, 0)

    arrived(refresh_ref, 5)
    arrived(cached_ref, 6)

    def sent(ref, n):
        pltpu.make_async_copy(ref, ref, send_sem.at[n]).wait()

    others = pl.ds(0, (shards - 1) * own)
    for n in (0, 1, 2, 5):
        sent(q_buf.at[others, :], n)
    sent(fresh_buf.at[pl.ds(0, shards - 1)], 3)
    sent(list_buf.at[pl.ds(0, shards - 1)], 4)
    sent(cached_buf.at[pl.ds(0, shards - 1)], 6)


def hand_over(refresh_in, cached_in, refresh_ref, cached_ref, sem):
    copies = [
        pltpu.make_async_copy(refresh_in, refresh_ref, sem.at[0]),
        pltpu.make_async_copy(cached_in, cached_ref, sem.at[1]),
    ]
    for copy in copies:
        copy.start()
    for copy in copies:
        copy.wait()


def per_device(
    queries, keys, values, fresh_queries, fresh_keys, fresh_values, masked_rows, masked_counts
):
    own, width = queries.shape
    slots = masked_rows.shape[1]
    shards = lax.axis_size("seq")
    tokens = shards * own
    bf16 = jnp.bfloat16
    hbm = pl.BlockSpec(memory_space=pltpu.HBM)
    anywhere = pl.BlockSpec(memory_space=pl.ANY)
    operands = [
        pltpu.with_memory_space_constraint(operand, pltpu.HBM)
        for operand in (
            queries,
            keys,
            values,
            fresh_queries,
            fresh_keys,
            fresh_values,
            masked_rows,
        )
    ]
    results = pl.pallas_call(
        functools.partial(kernel, shards),
        name="attention",
        out_shape=(
            jax.ShapeDtypeStruct((own, width), bf16),
            jax.ShapeDtypeStruct((slots, width), bf16),
        ),
        in_specs=[hbm] * 7 + [pl.BlockSpec(memory_space=pltpu.SMEM)],
        out_specs=(anywhere, anywhere),
        scratch_shapes=[
            pltpu.VMEM((tokens, HEAD_DIM), bf16),
            pltpu.VMEM((tokens, HEAD_DIM), bf16),
            pltpu.VMEM((tokens, 2 * HEAD_DIM), bf16),
            pltpu.VMEM((1, slots), jnp.int32),
            pltpu.VMEM((3, own, width), bf16),
            pltpu.VMEM((shards, slots, 3 * HEAD_DIM), bf16),
            pltpu.VMEM((shards, slots, 3 * HEAD_DIM), bf16),
            pltpu.VMEM((1, HEAD_DIM), jnp.int32),
            pltpu.VMEM((shards, 1, HEAD_DIM), jnp.int32),
            pltpu.VMEM((tokens, HEAD_DIM), bf16),
            pltpu.VMEM((shards, slots, HEAD_DIM), bf16),
            pltpu.SemaphoreType.DMA((4,)),
            pltpu.SemaphoreType.REGULAR((2,)),
            pltpu.SemaphoreType.DMA((7,)),
            pltpu.SemaphoreType.DMA((7,)),
        ],
        compiler_params=pltpu.CompilerParams(
            collective_id=0, has_side_effects=True, vmem_limit_bytes=VMEM_LIMIT
        ),
        cost_estimate=pl.CostEstimate(
            flops=6 * tokens * tokens * HEAD_DIM,
            bytes_accessed=12 * own * width,
            transcendentals=tokens * tokens * 3 // 2,
        ),
    )(
        *operands,
        masked_counts,
    )
    return pl.pallas_call(
        hand_over,
        name="hand_over",
        out_shape=tuple(jax.ShapeDtypeStruct(r.shape, r.dtype) for r in results),
        in_specs=[anywhere] * 2,
        out_specs=(hbm, hbm),
        scratch_shapes=[pltpu.SemaphoreType.DMA((2,))],
        compiler_params=pltpu.CompilerParams(vmem_limit_bytes=2**20),
    )(*results)


def solution(mesh):
    spread = P(("doc", "seq"), None)
    return jax.shard_map(
        per_device,
        mesh=mesh,
        in_specs=(spread,) * 7 + (P(("doc", "seq")),),
        out_specs=(spread, spread),
        check_vma=False,
    )
```

```python
import functools
import math

import jax
import jax.numpy as jnp
from jax import lax
from jax.experimental import pallas as pl
from jax.experimental.pallas import tpu as pltpu
from jax.sharding import PartitionSpec as P

HEAD_DIM = 128
PLANES = 8
VMEM_LIMIT = 40 * 2**20
MESH = pl.DeviceIdType.MESH
KEY_CHUNK = 256
EXP2_SCALE = math.log2(math.e) / math.sqrt(HEAD_DIM)


def attend(query_block, key_ref, value_ref):
    rows = query_block.shape[0]
    top = jnp.full((rows, 1), -jnp.inf, jnp.float32)
    total = jnp.zeros((rows, 2 * HEAD_DIM), jnp.float32)
    for c in range(0, key_ref.shape[0], KEY_CHUNK):
        scores = lax.dot_general(
            query_block,
            key_ref[pl.ds(c, KEY_CHUNK), :],
            (((1,), (1,)), ((), ())),
            preferred_element_type=jnp.float32,
        )
        new_top = jnp.maximum(top, jnp.max(scores, axis=-1, keepdims=True))
        powers = jnp.exp2((scores - new_top) * EXP2_SCALE).astype(jnp.bfloat16)
        total = total * jnp.exp2((top - new_top) * EXP2_SCALE) + jnp.dot(
            powers, value_ref[pl.ds(c, KEY_CHUNK), :], preferred_element_type=jnp.float32
        )
        top = new_top
    return total[:, :HEAD_DIM] / total[:, HEAD_DIM:]


def kernel(
    shards,
    q_ref,
    k_ref,
    v_ref,
    fq_ref,
    fk_ref,
    fv_ref,
    rows_ref,
    count_ref,
    refresh_ref,
    cached_ref,
    q_buf,
    k_buf,
    v_buf,
    rows_own,
    fresh_own,
    fresh_out,
    fresh_buf,
    list_out,
    list_buf,
    refresh_buf,
    cached_buf,
    load_sem,
    ready_sem,
    send_sem,
    recv_sem,
):
    me = lax.axis_index("seq")
    width = shards // PLANES
    own = q_ref.shape[0]
    slots = rows_ref.shape[1]

    def plane(i):
        step = PLANES // 2 + lax.div(i + 1, 2) * (1 - 2 * lax.rem(i, 2))
        return lax.rem(lax.div(me, width) + step, PLANES)

    def peer(i):
        reach = PLANES - 1
        far = lax.div(i, reach) < width
        step = jnp.where(far, lax.div(i, reach) + 1, i - reach * width + 1)
        x = lax.rem(lax.rem(me, width) + step, width)
        return plane(jnp.where(far, lax.rem(i, reach), reach)) * width + x

    def early_plane(i):
        half = PLANES // 2
        turn = lax.rem(i, half)
        step = half // 2 + lax.div(turn + 1, 2) * (1 - 2 * lax.rem(turn, 2))
        return lax.div(i, half) * half + lax.rem(lax.rem(lax.div(me, width), half) + step, half)

    def columns(head):
        return pl.ds(pl.multiple_of(head * HEAD_DIM, HEAD_DIM), HEAD_DIM)

    def rows_of(shard):
        return pl.ds(pl.multiple_of(shard * own, own), own)

    def device(dz, dx):
        z = lax.rem(lax.div(me, width) + dz, PLANES)
        return z * width + lax.rem(lax.rem(me, width) + dx, width)

    def signal(sem, dz, dx):
        pl.semaphore_signal(
            sem, inc=1, device_id={"seq": device(dz, dx)}, device_id_type=MESH
        )

    plane_mates = [(0, dx) for dx in range(1, width)]
    column_far, column_near = [(2, 0), (PLANES - 2, 0)], [(1, 0), (PLANES - 1, 0)]
    barrier = pltpu.get_barrier_semaphore()
    column_most = [(PLANES // 2, 0), (PLANES // 2 - 1, 0), (PLANES // 2 + 1, 0)]
    for place in column_most + column_far + column_near + plane_mates:
        signal(barrier, *place)

    loads = [
        pltpu.make_async_copy(ref, fresh_own.at[i], load_sem.at[i])
        for i, ref in enumerate((fq_ref, fk_ref, fv_ref))
    ]
    loads.append(pltpu.make_async_copy(rows_ref, rows_own, load_sem.at[3]))
    for load in loads:
        load.start()

    stage_a = ((k_ref, k_buf, 0), (v_ref, v_buf, 1), (q_ref, q_buf, 2))

    def send_a(n, places, columns_on):
        ref, buf, _ = stage_a[n]

        def one(c, carry):
            for dz, dx in places:
                to = device(dz, dx + c)
                pltpu.make_async_remote_copy(
                    src_ref=ref.at[:, columns(to)],
                    dst_ref=buf.at[rows_of(me), pl.ds(0, HEAD_DIM)],
                    send_sem=send_sem.at[n],
                    recv_sem=recv_sem.at[n],
                    device_id={"seq": to},
                    device_id_type=MESH,
                ).start()
            return carry

        lax.fori_loop(*columns_on, one, 0)

    own_column, other_columns, all_columns = (0, 1), (1, width), (0, width)
    near = column_far + column_near
    far = [(PLANES // 2, 0), (PLANES // 2 - 1, 0), (PLANES // 2 + 1, 0)]

    pl.semaphore_wait(barrier, len(far) + len(near) + len(plane_mates))
    for place in plane_mates:
        signal(ready_sem.at[0], *place)
    send_a(0, far, own_column)
    send_a(0, near, own_column)
    send_a(1, near, own_column)
    pl.semaphore_wait(ready_sem.at[0], len(plane_mates))
    send_a(0, near, other_columns)
    send_a(0, far, other_columns)
    send_a(1, far, own_column)
    send_a(1, far + near, other_columns)
    send_a(2, far + near, all_columns)
    for n in range(3):
        send_a(n, [(0, 0)], other_columns)
    for ref, buf, n in stage_a:
        pltpu.make_async_copy(
            ref.at[:, columns(me)], buf.at[rows_of(me), pl.ds(0, HEAD_DIM)], recv_sem.at[n]
        ).start()

    for load in loads:
        load.wait()
    count = count_ref[0]
    lane = lax.broadcasted_iota(jnp.int32, (1, slots), 1)
    listed = rows_own[...]
    list_out[...] = jnp.full(list_out.shape, count, jnp.int32)
    list_out[0:1, 0:slots] = jnp.where(lane < count, listed, -1)
    pick = (lax.broadcasted_iota(jnp.int32, (own, slots), 0) == listed).astype(jnp.float32)
    pick = jnp.transpose(pick).astype(jnp.bfloat16)

    def gather(head, carry):
        for i in range(3):
            fresh_out[head, :, pl.ds(i * HEAD_DIM, HEAD_DIM)] = jnp.dot(
                pick, fresh_own[i, :, columns(head)], preferred_element_type=jnp.float32
            ).astype(jnp.bfloat16)
        return carry

    lax.fori_loop(0, shards, gather, 0)

    def send_b(i, carry):
        to = peer(i)
        for src, dst, n in (
            (fresh_out.at[to], fresh_buf.at[me], 3),
            (list_out, list_buf.at[me], 4),
        ):
            pltpu.make_async_remote_copy(
                src_ref=src,
                dst_ref=dst,
                send_sem=send_sem.at[n],
                recv_sem=recv_sem.at[n],
                device_id={"seq": to},
                device_id_type=MESH,
            ).start()
        return carry

    lax.fori_loop(0, shards - 1, send_b, 0)
    pltpu.make_async_copy(fresh_out.at[me], fresh_buf.at[me], recv_sem.at[3]).start()
    pltpu.make_async_copy(list_out, list_buf.at[me], recv_sem.at[4]).start()

    v_buf[:, HEAD_DIM:] = jnp.ones((v_buf.shape[0], HEAD_DIM), jnp.bfloat16)

    def arrived(ref, n):
        pltpu.make_async_copy(ref, ref, recv_sem.at[n]).wait()

    arrived(k_buf, 0)
    arrived(v_buf.at[:, pl.ds(0, HEAD_DIM)], 1)
    arrived(q_buf, 2)

    def send_home(src, dst, to, n):
        @pl.when(to != me)
        def _():
            pltpu.make_async_remote_copy(
                src_ref=src,
                dst_ref=dst,
                send_sem=send_sem.at[n],
                recv_sem=recv_sem.at[n],
                device_id={"seq": to},
                device_id_type=MESH,
            ).start()

        @pl.when(to == me)
        def _():
            pltpu.make_async_copy(src, dst, recv_sem.at[n]).start()

    eager = lax.rem(lax.axis_index("doc"), 2) == 0

    def send_refresh(first):
        for j in range(width):
            to = first + j
            send_home(refresh_buf.at[rows_of(to)], refresh_ref.at[:, columns(me)], to, 5)

    def refresh(i, carry):
        first = plane(i) * width
        block = pl.ds(pl.multiple_of(first * own, width * own), width * own)
        out = attend(q_buf[block, :], k_buf, v_buf)
        refresh_buf[block, :] = out.astype(jnp.bfloat16)

        @pl.when(eager)
        def _():
            send_refresh(first)

        return carry

    lax.fori_loop(0, PLANES, refresh, 0)

    @pl.when(jnp.logical_not(eager))
    def _():
        def late(i, carry):
            send_refresh(plane(i) * width)
            return carry

        lax.fori_loop(0, PLANES, late, 0)


    arrived(fresh_buf, 3)
    arrived(list_buf, 4)

    def update(i, carry):
        for j in range(width):
            shard = i * width + j
            at = list_buf[shard, 0:1, 0:slots]
            put = lax.broadcasted_iota(jnp.int32, (own, slots), 0) == at
            put = put.astype(jnp.float32)
            changed = jnp.max(put, axis=-1, keepdims=True) > 0.0
            new = jnp.dot(
                put.astype(jnp.bfloat16),
                fresh_buf[shard, :, HEAD_DIM:],
                preferred_element_type=jnp.float32,
            ).astype(jnp.bfloat16)
            block = rows_of(shard)
            k_buf[block, :] = jnp.where(changed, new[:, :HEAD_DIM], k_buf[block, :])
            v_buf[block, :HEAD_DIM] = jnp.where(
                changed, new[:, HEAD_DIM:], v_buf[block, :HEAD_DIM]
            )
        return carry

    lax.fori_loop(0, PLANES, update, 0)

    def cached(i, carry):
        firsts = [early_plane(2 * i + j) * width for j in range(2)]
        groups = [pl.ds(first, width) for first in firsts]
        query_block = jnp.concatenate([fresh_buf[g, :, 0:HEAD_DIM] for g in groups])
        out = attend(query_block.reshape(-1, HEAD_DIM), k_buf, v_buf)
        out = out.reshape(2, width, slots, HEAD_DIM)
        slot = lax.broadcasted_iota(jnp.int32, out.shape[1:], 1)
        for j, group in enumerate(groups):
            live = slot < list_buf[group, 0:1, HEAD_DIM - 1 :]
            cached_buf[group, :, :] = jnp.where(live, out[j], 0.0).astype(jnp.bfloat16)
        for first in firsts:
            for j in range(width):
                to = first + j
                send_home(cached_buf.at[to], cached_ref.at[:, columns(me)], to, 6)
        return carry

    lax.fori_loop(0, PLANES // 2, cached, 0)

    arrived(refresh_ref, 5)
    arrived(cached_ref, 6)

    def sent(ref, n):
        pltpu.make_async_copy(ref, ref, send_sem.at[n]).wait()

    others = pl.ds(0, (shards - 1) * own)
    for n in (0, 1, 2, 5):
        sent(q_buf.at[others, :], n)
    sent(fresh_buf.at[pl.ds(0, shards - 1)], 3)
    sent(list_buf.at[pl.ds(0, shards - 1)], 4)
    sent(cached_buf.at[pl.ds(0, shards - 1)], 6)


def hand_over(refresh_in, cached_in, refresh_ref, cached_ref, sem):
    copies = [
        pltpu.make_async_copy(refresh_in, refresh_ref, sem.at[0]),
        pltpu.make_async_copy(cached_in, cached_ref, sem.at[1]),
    ]
    for copy in copies:
        copy.start()
    for copy in copies:
        copy.wait()


def per_device(
    queries, keys, values, fresh_queries, fresh_keys, fresh_values, masked_rows, masked_counts
):
    own, width = queries.shape
    slots = masked_rows.shape[1]
    shards = lax.axis_size("seq")
    tokens = shards * own
    bf16 = jnp.bfloat16
    hbm = pl.BlockSpec(memory_space=pltpu.HBM)
    anywhere = pl.BlockSpec(memory_space=pl.ANY)
    operands = [
        pltpu.with_memory_space_constraint(operand, pltpu.HBM)
        for operand in (
            queries,
            keys,
            values,
            fresh_queries,
            fresh_keys,
            fresh_values,
            masked_rows,
        )
    ]
    results = pl.pallas_call(
        functools.partial(kernel, shards),
        name="attention",
        out_shape=(
            jax.ShapeDtypeStruct((own, width), bf16),
            jax.ShapeDtypeStruct((slots, width), bf16),
        ),
        in_specs=[hbm] * 7 + [pl.BlockSpec(memory_space=pltpu.SMEM)],
        out_specs=(anywhere, anywhere),
        scratch_shapes=[
            pltpu.VMEM((tokens, HEAD_DIM), bf16),
            pltpu.VMEM((tokens, HEAD_DIM), bf16),
            pltpu.VMEM((tokens, 2 * HEAD_DIM), bf16),
            pltpu.VMEM((1, slots), jnp.int32),
            pltpu.VMEM((3, own, width), bf16),
            pltpu.VMEM((shards, slots, 3 * HEAD_DIM), bf16),
            pltpu.VMEM((shards, slots, 3 * HEAD_DIM), bf16),
            pltpu.VMEM((1, HEAD_DIM), jnp.int32),
            pltpu.VMEM((shards, 1, HEAD_DIM), jnp.int32),
            pltpu.VMEM((tokens, HEAD_DIM), bf16),
            pltpu.VMEM((shards, slots, HEAD_DIM), bf16),
            pltpu.SemaphoreType.DMA((4,)),
            pltpu.SemaphoreType.REGULAR((1,)),
            pltpu.SemaphoreType.DMA((7,)),
            pltpu.SemaphoreType.DMA((7,)),
        ],
        compiler_params=pltpu.CompilerParams(
            collective_id=0, has_side_effects=True, vmem_limit_bytes=VMEM_LIMIT
        ),
        cost_estimate=pl.CostEstimate(
            flops=6 * tokens * tokens * HEAD_DIM,
            bytes_accessed=12 * own * width,
            transcendentals=tokens * tokens * 3 // 2,
        ),
    )(
        *operands,
        masked_counts,
    )
    return pl.pallas_call(
        hand_over,
        name="hand_over",
        out_shape=tuple(jax.ShapeDtypeStruct(r.shape, r.dtype) for r in results),
        in_specs=[anywhere] * 2,
        out_specs=(hbm, hbm),
        scratch_shapes=[pltpu.SemaphoreType.DMA((2,))],
        compiler_params=pltpu.CompilerParams(vmem_limit_bytes=2**20),
    )(*results)


def solution(mesh):
    spread = P(("doc", "seq"), None)
    return jax.shard_map(
        per_device,
        mesh=mesh,
        in_specs=(spread,) * 7 + (P(("doc", "seq")),),
        out_specs=(spread, spread),
        check_vma=False,
    )
```
